32 devices in a mesh: ctx: 8 (over y, x, core), tp: 4 (over z).
Axes of the slice: x: 2, y: 2, z: 4, core: 2. Of those that a mesh axis runs over, the one named last changes fastest.
Arguments:
- tokens: bfloat16 [2048, 8192], P('ctx', 'tp'), may hold values from -6 to 6
- frozen: bfloat16 [2048, 3, 8192], P('ctx', None, 'tp'), may hold values from -3 to 3
- cotangent: bfloat16 [2048, 8192], P('ctx', 'tp'), may hold values from -0.119628906 to 0.119628906
- adapter_down_weight: bfloat16 [16, 8192], P(None, 'tp'), may hold values from -0.0625 to 0.0625
- adapter_up_weight: bfloat16 [16, 3, 8192], P(None, None, 'tp'), may hold values from -0.75 to 0.75
- short_depthwise_filter: bfloat16 [3, 3, 8192], P(None, None, 'tp'), may hold values from -3.5 to 3.5
- long_group_filter: bfloat16 [512, 128], P('tp'), may hold values from -8 to 8
- skip_direct_scale: float32 [8192], P('tp'), may hold values from -3 to 3
- document_lengths: int32 [16], replicated, may hold values from 1 to 1024, 2048 in all
- window_row_position: int32 [2048], P('ctx'), may hold values from 0 to 2047, as said below
Outputs:
- mixer_out: bfloat16 [2048, 8192], P('ctx', 'tp')
- grad_down: float32 [16, 8192], P(None, 'tp')
- up_gradient: float32 [16, 3, 8192], P(None, None, 'tp')
- grad_short: float32 [3, 3, 8192], P(None, None, 'tp')
- grad_long: float32 [512, 128], P('tp')
- grad_skip: float32 [8192], P('tp')
The draws below stay inside these ranges and needn't reach their ends.
Inputs may be any that keep to these rules, and one draw needn't show every extreme that they name: `window_row_position`: a permutation of the window's positions; the rows of one loader device (one index of ctx) go to each context shard (places j * 256 to (j + 1) * 256 - 1) in a count of 0, 32 or 64, and in a count of 64 to at least one shard. `document_lengths`: the documents lie end to end in the window in this order; the lengths sum to 2048.
All inputs are finite; a program needn't handle non-finite values.
Results may differ from the reference program's by a relative error of at most 0.0055.
The reference program's roundings to bfloat16 on the way count: a program that leaves them out, or rounds other values in their place, can miss the bound.
Values may be sent and summed in bfloat16 or wider, within the bound.
A program may use at most 128 MiB of HBM per device.

```python
import math
import jax
import jax.numpy as jnp
import numpy as np
from jax import lax

MIXER_WIDTH = 8192
ADAPTER_RANK = 16
TAPS = 128
SHORT_TAPS = 3
TOK_DEV = 256
WINDOW = 2048
GROUPS = 512
DOCS = 16
LONGEST = 1024
N_TP = 4


def draw_window_row_position(key, part):
    shards = WINDOW // TOK_DEV
    share_count = TOK_DEV // shards
    key_order, key_place, key_slots = jax.random.split(key, 3)
    shard_ids = jnp.arange(shards, dtype=jnp.int32)
    ordering = jax.random.permutation(key_order, shards).astype(jnp.int32)
    following = jnp.roll(ordering, -1)
    plus_one = (shard_ids[None, :] == ordering[:, None]).astype(jnp.int32)
    minus_one = (shard_ids[None, :] == following[:, None]).astype(jnp.int32)
    counts = share_count * (1 + plus_one - minus_one)

    def spread(count_row):
        return jnp.repeat(shard_ids, count_row, total_repeat_length=TOK_DEV)
    destination = jax.vmap(spread)(counts).reshape(-1).astype(jnp.int32)
    matches = (destination[:, None] == shard_ids[None, :]).astype(jnp.int32)
    within = jnp.sum(jnp.cumsum(matches, axis=0) * matches, axis=1) - 1
    placements = jax.vmap(lambda single: jax.random.permutation(single, TOK_DEV))(jax.random.split(key_place, shards)).astype(jnp.int32)
    target = destination * TOK_DEV + placements[destination, within]
    shuffles = jax.vmap(lambda single: jax.random.permutation(single, TOK_DEV))(jax.random.split(key_slots, shards)).astype(jnp.int32)
    arranged = jnp.take_along_axis(target.reshape(shards, TOK_DEV), shuffles, axis=1)
    return arranged.reshape(-1).astype(jnp.int32)


def draw_long_group_filter(key, part):
    key_taps, key_rate, key_scale = jax.random.split(key, 3)
    lags = jnp.arange(TAPS, dtype=jnp.float32)
    rates = jnp.exp(jax.random.uniform(key_rate, (GROUPS, 1), jnp.float32, math.log(8.0), math.log(512.0)))
    values = jnp.clip(jax.random.normal(key_taps, (GROUPS, TAPS), jnp.float32), -4.0, 4.0)
    envelope = jnp.exp(-lags[None, :] / rates)
    scales = jnp.exp(jax.random.uniform(key_scale, (GROUPS, 1), jnp.float32, math.log(0.5), math.log(2.0)))
    filtered = values * envelope * scales / jnp.sqrt(jnp.sum(envelope * envelope, axis=1, keepdims=True))
    return filtered.astype(jnp.bfloat16)


def shard_levels(own_key, dims, cuts, low, top_value):
    loudness = 1.0
    for dim, shards_of in cuts:
        heights = jax.random.uniform(jax.random.fold_in(jax.random.fold_in(own_key, 6), dim), (shards_of,), jnp.float32, low / len(cuts), top_value / len(cuts))
        loudness = loudness * jnp.repeat(jnp.exp(heights), dims[dim] // shards_of).reshape((-1,) + (1,) * (len(dims) - 1 - dim))
    return loudness


def split_up(count, total, bound, slope):
    loads = [(1 << 20) // math.isqrt(grade ** slope) + 1 for grade in range(2, count + 1)]
    surplus, holding = total - bound - (count - 1), [1] * (count - 1)
    while surplus > 0:
        movable = [i for i in range(count - 1) if holding[i] < bound]
        pool, remaining = sum([loads[i] for i in movable]), surplus
        for i in movable:
            addition = min(bound - holding[i], max(1, remaining * loads[i] // pool), surplus)
            holding[i] = holding[i] + addition
            surplus = surplus - addition
    return np.array([bound] + holding)


def ragged(key, amount, total, most, lean):
    if amount == 2:
        one = jax.random.randint(key, (), max(1, total - most), min(most, total - 1) + 1)
        return jnp.stack([one, total - one])
    lengths = jnp.asarray(split_up(amount, total, most, lean), jnp.int32)
    couples = (amount - 1) // 2
    donor, receiver = lengths[1:1 + 2 * couples:2], lengths[2:2 + 2 * couples:2]
    room = jnp.minimum(donor - 1, most - receiver)
    passed = jax.random.randint(jax.random.fold_in(key, 1), (couples,), 0, 1 << 20) % (room + 1)
    lengths = lengths.at[1:1 + 2 * couples:2].set(donor - passed).at[2:2 + 2 * couples:2].set(receiver + passed)
    return lengths[jax.random.permutation(jax.random.fold_in(key, 2), amount)]


def noise(rng, dims, scale, most, cuts=(), kind=jnp.bfloat16):
    drawn = jax.random.normal(rng, dims, jnp.float32) * scale
    if len(cuts) > 0:
        drawn = shard_levels(rng, dims, cuts, -0.22, 0.18) * drawn
    return jnp.clip(drawn, min=-most, max=most).astype(kind)


def setup_inputs(seed: int = 0) -> dict:
    keys = jax.random.split(jax.random.key(seed), 11)
    tokens = noise(keys[0], (WINDOW, MIXER_WIDTH), 1.0, 6.0, ((0, 8), (1, 4)))
    frozen = noise(keys[1], (WINDOW, 3, MIXER_WIDTH), 0.5, 3.0, ((0, 8), (2, 4)))
    cotangent = noise(keys[2], (WINDOW, MIXER_WIDTH), 0.02, 0.119628906, ((0, 8), (1, 4)))
    adapter_down_weight = noise(keys[3], (ADAPTER_RANK, MIXER_WIDTH), MIXER_WIDTH ** -0.5, 0.0625, ((1, 4),))
    adapter_up_weight = noise(keys[4], (ADAPTER_RANK, 3, MIXER_WIDTH), (4 * ADAPTER_RANK) ** -0.5, 0.75, ((2, 4),))
    short_depthwise_filter = noise(keys[5], (SHORT_TAPS, 3, MIXER_WIDTH), SHORT_TAPS ** -0.5, 3.5, ((2, 4),))
    long_group_filter = draw_long_group_filter(jax.random.fold_in(keys[10], 71), 0)
    skip_direct_scale = noise(keys[7], (MIXER_WIDTH,), 0.5, 3.0, ((0, 4),), jnp.float32)
    document_lengths = ragged(keys[8], DOCS, WINDOW, LONGEST, 2).astype(jnp.int32)
    window_row_position = draw_window_row_position(jax.random.fold_in(keys[10], 71), 0)
    return dict(tokens=tokens, frozen=frozen, cotangent=cotangent, adapter_down_weight=adapter_down_weight, adapter_up_weight=adapter_up_weight, short_depthwise_filter=short_depthwise_filter, long_group_filter=long_group_filter, skip_direct_scale=skip_direct_scale, document_lengths=document_lengths, window_row_position=window_row_position)


def doc_offsets(positions, document_lengths):
    doc_ends = jnp.cumsum(document_lengths).astype(jnp.int32)
    starts = (doc_ends - document_lengths).astype(jnp.int32)
    clipped = jnp.maximum(positions, 0).astype(jnp.int32)
    begins = jnp.max(jnp.where(starts[None, :] <= clipped[:, None], starts[None, :], 0), axis=1)
    return (clipped - begins).astype(jnp.int32)


def tap_mask(offsets, shift_tap, ndim):
    return (shift_tap <= offsets).astype(jnp.float32).reshape((-1,) + (1,) * (ndim - 1))


def rounded_length(value):
    return lax.optimization_barrier(value.astype(jnp.bfloat16)).astype(jnp.float32)


def short_forward(pre_rows, filter_taps, offsets):
    length = pre_rows.shape[0]
    taps = filter_taps.shape[0]
    reach = taps - 1
    padded = jnp.concatenate([jnp.zeros((reach,) + pre_rows.shape[1:], jnp.float32), pre_rows])
    running = jnp.zeros(pre_rows.shape, jnp.float32)
    for shift_tap in range(taps):
        running = running + filter_taps[shift_tap] * padded[reach - shift_tap:reach - shift_tap + length] * tap_mask(offsets, shift_tap, pre_rows.ndim)
    return running


def short_adjoint(back_rows, filter_taps, offsets):
    length = back_rows.shape[0]
    taps = filter_taps.shape[0]
    reach = taps - 1
    running = jnp.zeros(back_rows.shape, jnp.float32)
    for shift_tap in range(taps):
        masked = back_rows * tap_mask(offsets, shift_tap, back_rows.ndim)
        padded = jnp.concatenate([masked, jnp.zeros((reach,) + back_rows.shape[1:], jnp.float32)])
        running = running + filter_taps[shift_tap] * padded[shift_tap:shift_tap + length]
    return running


def short_gradient(back_rows, pre_rows, offsets, taps):
    length = pre_rows.shape[0]
    reach = taps - 1
    padded = jnp.concatenate([jnp.zeros((reach,) + pre_rows.shape[1:], jnp.float32), pre_rows])
    collected = []
    for shift_tap in range(taps):
        shifted = padded[reach - shift_tap:reach - shift_tap + length]
        collected.append(jnp.sum(back_rows * shifted * tap_mask(offsets, shift_tap, pre_rows.ndim), axis=0))
    return jnp.stack(collected)


def long_forward(product_rows, filter_bank, offsets):
    length, channels = product_rows.shape
    padded = jnp.concatenate([jnp.zeros((128, channels), jnp.float32), product_rows])

    def one_tap(shift_tap, running):
        shift_tap = shift_tap.astype(jnp.int32)
        column = jnp.repeat(lax.dynamic_index_in_dim(filter_bank, shift_tap, 1, keepdims=False), 16)
        shifted = lax.dynamic_slice_in_dim(padded, (128 - shift_tap).astype(jnp.int32), length, 0)
        tap_gate = (shift_tap <= offsets).astype(jnp.float32)[:, None]
        return running + column[None, :] * shifted * tap_gate

    return lax.fori_loop(0, 128, one_tap, jnp.zeros((length, channels), jnp.float32))


def long_adjoint(back_rows, filter_bank, offsets):
    length, channels = back_rows.shape

    def one_tap(shift_tap, running):
        shift_tap = shift_tap.astype(jnp.int32)
        column = jnp.repeat(lax.dynamic_index_in_dim(filter_bank, shift_tap, 1, keepdims=False), 16)
        tap_gate = (shift_tap <= offsets).astype(jnp.float32)[:, None]
        padded = jnp.concatenate([back_rows * tap_gate, jnp.zeros((128, channels), jnp.float32)])
        shifted = lax.dynamic_slice_in_dim(padded, shift_tap, length, 0)
        return running + column[None, :] * shifted

    return lax.fori_loop(0, 128, one_tap, jnp.zeros((length, channels), jnp.float32))


def long_gradient(back_rows, product_rows, offsets):
    length, channels = product_rows.shape
    padded = jnp.concatenate([jnp.zeros((128, channels), jnp.float32), product_rows])

    def one_tap(shift_tap, running):
        shift_tap = shift_tap.astype(jnp.int32)
        shifted = lax.dynamic_slice_in_dim(padded, (128 - shift_tap).astype(jnp.int32), length, 0)
        tap_gate = (shift_tap <= offsets).astype(jnp.float32)[:, None]
        per_channel = jnp.sum(back_rows * shifted * tap_gate, axis=0)
        per_group = per_channel.reshape(channels // 16, 16).sum(axis=1)
        return lax.dynamic_update_slice(running, per_group[:, None], (jnp.int32(0), shift_tap))

    return lax.fori_loop(0, 128, one_tap, jnp.zeros((channels // 16, 128), jnp.float32))


def reference(tokens, frozen, cotangent, adapter_down_weight, adapter_up_weight, short_depthwise_filter, long_group_filter, skip_direct_scale, document_lengths, window_row_position):
    width_tile_block = MIXER_WIDTH // N_TP
    rank_total = adapter_down_weight.shape[0]
    taps = short_depthwise_filter.shape[0]
    packed_token_rows = jnp.zeros((WINDOW, MIXER_WIDTH), jnp.bfloat16).at[window_row_position].set(tokens)
    packed_frozen = jnp.zeros((WINDOW, 3, MIXER_WIDTH), jnp.bfloat16).at[window_row_position].set(frozen)
    offsets = doc_offsets(jnp.arange(WINDOW, dtype=jnp.int32), document_lengths)
    lowrank_product = jnp.dot(adapter_down_weight, packed_token_rows.T, preferred_element_type=jnp.float32).astype(jnp.bfloat16)
    lowrank_single_float = lowrank_product.astype(jnp.float32)

    frozen_parts = packed_frozen.reshape(WINDOW, 3, N_TP, width_tile_block).transpose(2, 0, 1, 3)
    cot_parts = cotangent.reshape(WINDOW, N_TP, width_tile_block).transpose(1, 0, 2)
    up_weight_pieces = adapter_up_weight.reshape(rank_total, 3, N_TP, width_tile_block).transpose(2, 0, 1, 3)
    short_parts = short_depthwise_filter.reshape(taps, 3, N_TP, width_tile_block).transpose(2, 0, 1, 3)
    long_parts = long_group_filter.reshape(N_TP, GROUPS // N_TP, 128)
    skip_parts = skip_direct_scale.reshape(N_TP, width_tile_block)

    def one_block(carried_state, pieces):
        frozen_piece, cot_part, up_part, short_part, long_part, skip_part = pieces
        up_weight_single_float = up_part.astype(jnp.float32)
        short_float = short_part.astype(jnp.float32)
        long_float = long_part.astype(jnp.float32)
        before_convolution = rounded_length(frozen_piece.astype(jnp.float32) + jnp.einsum('ed,ejg->djg', lowrank_single_float, up_weight_single_float))
        post_conv = rounded_length(short_forward(before_convolution, short_float, offsets))
        query_rows = post_conv[:, 0]
        key_rows = post_conv[:, 1]
        value_rows = post_conv[:, 2]
        product = rounded_length(key_rows * value_rows)
        convolved = long_forward(product, long_float, offsets)
        mixer_part = (query_rows * (convolved + skip_part[None, :] * product)).astype(jnp.bfloat16)
        grad_float = cot_part.astype(jnp.float32)
        gated_back = grad_float * query_rows
        back_conv = rounded_length(gated_back)
        product_back = long_adjoint(back_conv, long_float, offsets) + skip_part[None, :] * gated_back
        grad_long_part = long_gradient(back_conv, product, offsets)
        grad_skip_part = jnp.sum(gated_back * product, axis=0)
        query_back = grad_float * (convolved + skip_part[None, :] * product)
        back_post = rounded_length(jnp.stack([query_back, product_back * value_rows, product_back * key_rows], axis=1))
        gradient_before_filter = rounded_length(short_adjoint(back_post, short_float, offsets))
        grad_short_part = short_gradient(back_post, before_convolution, offsets, taps)
        up_gradient_piece = jnp.einsum('kp,pme->kme', lowrank_single_float, gradient_before_filter)
        carried_state = carried_state + jnp.einsum('ldx,idx->li', up_weight_single_float, gradient_before_filter)
        return carried_state, (mixer_part, up_gradient_piece, grad_short_part, grad_long_part, grad_skip_part)

    start = jnp.zeros((rank_total, WINDOW), jnp.float32)
    carried_state, stacked = lax.scan(one_block, start, (frozen_parts, cot_parts, up_weight_pieces, short_parts, long_parts, skip_parts))
    mixer_parts, grad_up_parts, grad_short_parts, grad_long_parts, grad_skip_parts = stacked
    back_low = carried_state.astype(jnp.bfloat16)
    grad_down = jnp.dot(back_low, packed_token_rows, preferred_element_type=jnp.float32)
    mixer_out = mixer_parts.transpose(1, 0, 2).reshape(WINDOW, MIXER_WIDTH)
    up_gradient = grad_up_parts.transpose(1, 2, 0, 3).reshape(rank_total, 3, MIXER_WIDTH)
    grad_short = grad_short_parts.transpose(1, 2, 0, 3).reshape(taps, 3, MIXER_WIDTH)
    grad_long = grad_long_parts.reshape(GROUPS, 128)
    grad_skip = grad_skip_parts.reshape(MIXER_WIDTH)
    return (mixer_out, grad_down, up_gradient, grad_short, grad_long, grad_skip)
```

```python
import functools

import jax
import jax.numpy as jnp
from jax import lax
from jax.experimental import pallas as pl
from jax.experimental.pallas import tpu as pltpu
from jax.sharding import PartitionSpec as P

EDGE = 16
LANES = 128


def fdot(left, right, contract=((1,), (0,))):
    return lax.dot_general(left, right, (contract, ((), ())), preferred_element_type=jnp.float32)


def doc_starts(pos, lengths_ref):
    begins = jnp.zeros_like(pos)
    running = jnp.int32(0)
    for doc in range(lengths_ref.shape[0]):
        begins = jnp.where(pos >= running, running, begins)
        running = running + lengths_ref[doc]
    return begins


def core_kernel(
    lengths_ref,
    frozen_ref,
    low_ref,
    place_ref,
    cot_ref,
    up_ref,
    short_ref,
    taps_f_ref,
    taps_b_ref,
    skip_ref,
    out_ref,
    up_grad_ref,
    short_grad_ref,
    long_grad_ref,
    skip_grad_ref,
    back_low_ref,
    rhs,
    pre,
    low_win,
    post,
    prod,
    back,
    back_post,
    bank_f,
    bank_b,
    pair_acc,
    start_col,
    start_row,
):
    n, c = cot_ref.shape
    groups, wide = taps_f_ref.shape
    taps = wide // 2
    per = c // groups
    shards, kinds, rows, _ = frozen_ref.shape
    width = kinds * c
    blocks = n // taps
    shorts = short_ref.shape[0]
    f32, bf16 = jnp.float32, jnp.bfloat16

    start_col[...] = doc_starts(
        lax.broadcasted_iota(jnp.int32, start_col.shape, 0), lengths_ref
    )
    start_row[...] = doc_starts(
        lax.broadcasted_iota(jnp.int32, start_row.shape, 1), lengths_ref
    )

    for g in range(groups):
        span = slice(g * taps, (g + 1) * taps)
        for taps_ref, bank in ((taps_f_ref, bank_f), (taps_b_ref, bank_b)):
            line = jnp.broadcast_to(taps_ref[g : g + 1, :], (taps, wide))
            bank[span, :] = pltpu.roll(line, 0, 1, stride=1, stride_axis=0).astype(bf16)

    @pl.loop(0, shards)
    def _(j):
        at = pl.ds(pl.multiple_of(j * rows, rows), rows)
        low = low_ref[at, :]
        for a in range(kinds):
            cols = slice(a * c, (a + 1) * c)
            rhs[at, cols] = (frozen_ref[j, a].astype(f32) + fdot(low, up_ref[:, cols])).astype(bf16)
        rhs[at, width:] = low

    pre[:EDGE, :] = jnp.zeros((EDGE, width), bf16)
    tall = rows * 2

    @pl.loop(0, n // tall)
    def _(w):
        base = pl.multiple_of(w * tall, tall)
        spot = lax.broadcasted_iota(jnp.int32, (tall, n), 0) + base
        hot = jnp.where(place_ref[...] == spot, 1.0, 0.0).astype(bf16)
        moved = fdot(hot, rhs[...]).astype(bf16)
        pre[pl.ds(pl.multiple_of(base + EDGE, EDGE), tall), :] = moved[:, :width]
        low_win[pl.ds(base, tall), :] = moved[:, width:]

    prod[:taps, :] = jnp.zeros((taps, c), bf16)
    back[n:, :] = jnp.zeros((taps, c), bf16)

    @pl.loop(0, blocks)
    def _(b):
        base = pl.multiple_of(b * taps, taps)
        at = pl.ds(base, taps)
        ext = pre[pl.ds(base, taps + EDGE), :].astype(f32)
        off = lax.broadcasted_iota(jnp.int32, (taps, 1), 0) + base - start_col[at, :]
        total = jnp.zeros((taps, width), f32)
        for s in range(shorts):
            gate = (off >= s).astype(f32)
            total = total + short_ref[s : s + 1, :] * ext[EDGE - s : EDGE - s + taps] * gate
        rounded = total.astype(bf16)
        post[at, :] = rounded
        rounded = rounded.astype(f32)
        prod[pl.ds(pl.multiple_of(base + taps, taps), taps), :] = (
            rounded[:, c : 2 * c] * rounded[:, 2 * c :]
        ).astype(bf16)
        back[at, :] = (cot_ref[at, :].astype(f32) * rounded[:, :c]).astype(bf16)

    pair_acc[...] = jnp.zeros_like(pair_acc)
    skip_grad_ref[...] = jnp.zeros_like(skip_grad_ref)
    back_post[n:, :] = jnp.zeros((EDGE, width), bf16)
    lane_group = lax.broadcasted_iota(jnp.int32, (taps, c), 1) // per

    def pick(stacked):
        chosen = stacked[:taps]
        for g in range(1, groups):
            chosen = jnp.where(lane_group == g, stacked[g * taps : (g + 1) * taps], chosen)
        return chosen

    @pl.loop(0, blocks)
    def _(b):
        base = pl.multiple_of(b * taps, taps)
        at = pl.ds(base, taps)
        window = prod[pl.ds(base, 2 * taps), :]
        ahead = back[pl.ds(base, 2 * taps), :]
        col_pos = lax.broadcasted_iota(jnp.int32, (taps, wide), 1) + (base - taps)
        same_f = col_pos >= start_col[at, :]
        gate_f = jnp.where(same_f, 1.0, 0.0)
        row_pos = lax.broadcasted_iota(jnp.int32, (taps, wide), 0) + base
        same_b = row_pos >= start_row[:, pl.ds(base, wide)]
        gate_b = jnp.where(same_b, 1.0, 0.0).astype(bf16)
        many_f = jnp.concatenate([gate_f.astype(bf16)] * groups, axis=0)
        many_b = jnp.concatenate([gate_b] * groups, axis=0)
        conv = pick(fdot(bank_f[...] * many_f, window))
        spread = pick(fdot(bank_b[...] * many_b, ahead))
        here = ahead[:taps]
        split = jnp.concatenate(
            [jnp.where(lane_group == g, here, jnp.zeros_like(here)) for g in range(groups)], axis=0
        )
        pairs = fdot(split, window, ((1,), (1,)))
        for g in range(groups):
            span = slice(g * taps, (g + 1) * taps)
            pair_acc[span, :] += pairs[span] * gate_f
        product = window[taps:].astype(f32)
        cot = cot_ref[at, :].astype(f32)
        query = post[at, :c].astype(f32)
        key = post[at, c : 2 * c].astype(f32)
        value = post[at, 2 * c :].astype(f32)
        gated = cot * query
        skip = skip_ref[...]
        direct = conv + skip * product
        out_ref[at, :] = (query * direct).astype(bf16)
        product_back = spread + skip * gated
        skip_grad_ref[...] += jnp.sum(gated * product, axis=0, keepdims=True)
        back_post[at, :c] = (cot * direct).astype(bf16)
        back_post[at, c : 2 * c] = (product_back * value).astype(bf16)
        back_post[at, 2 * c :] = (product_back * key).astype(bf16)

    bits = taps.bit_length() - 1
    line_id = lax.broadcasted_iota(jnp.int32, (taps, wide), 0)

    @pl.loop(0, groups)
    def _(g):
        square = pair_acc[pl.ds(pl.multiple_of(g * taps, taps), taps), :]
        for bit in range(bits):
            step = 1 << bit
            square = jnp.where((line_id // step) % 2 == 1, pltpu.roll(square, wide - step, 1), square)
        long_grad_ref[pl.ds(g, 1), :] = jnp.sum(square, axis=0, keepdims=True)

    short_grad_ref[...] = jnp.zeros_like(short_grad_ref)

    @pl.loop(0, blocks)
    def _(b):
        base = pl.multiple_of(b * taps, taps)
        at = pl.ds(base, taps)
        ext = pre[pl.ds(base, taps + EDGE), :].astype(f32)
        back_ext = back_post[pl.ds(base, taps + EDGE), :].astype(f32)
        off = (
            lax.broadcasted_iota(jnp.int32, (taps + EDGE, 1), 0)
            + base
            - start_col[pl.ds(base, taps + EDGE), :]
        )
        total = jnp.zeros((taps, width), f32)
        for s in range(shorts):
            masked = back_ext * (off >= s).astype(f32)
            total = total + short_ref[s : s + 1, :] * masked[s : s + taps]
            short_grad_ref[s : s + 1, :] += jnp.sum(
                masked[:taps] * ext[EDGE - s : EDGE - s + taps], axis=0, keepdims=True
            )
        rhs[at, :width] = total.astype(bf16)

    rank = up_grad_ref.shape[0]
    back_pre = rhs[:, :width]
    up_grad_ref[...] = fdot(low_win[...], back_pre, ((0,), (0,)))[:rank]
    back_low_ref[...] = fdot(up_ref[:rank, :], back_pre, ((1,), (1,)))


def core(lengths, frozen, low, place, cot, up, short, taps_f, taps_b, skip, rank):
    n, c = cot.shape
    groups, wide = taps_f.shape
    taps = wide // 2
    kinds = frozen.shape[1]
    width = kinds * c
    f32, bf16 = jnp.float32, jnp.bfloat16
    vmem = pl.BlockSpec(memory_space=pltpu.VMEM)
    shape = jax.ShapeDtypeStruct
    return pl.pallas_call(
        core_kernel,
        out_shape=(
            shape((n, c), bf16),
            shape((rank, width), f32),
            shape((short.shape[0], width), f32),
            shape((groups, wide), f32),
            shape((1, c), f32),
            shape((rank, n), f32),
        ),
        in_specs=[pl.BlockSpec(memory_space=pltpu.SMEM)] + [vmem] * 9,
        out_specs=(vmem,) * 6,
        scratch_shapes=[
            pltpu.VMEM((n, width + LANES), bf16),
            pltpu.VMEM((n + EDGE, width), bf16),
            pltpu.VMEM((n, LANES), bf16),
            pltpu.VMEM((n, width), bf16),
            pltpu.VMEM((n + taps, c), bf16),
            pltpu.VMEM((n + taps, c), bf16),
            pltpu.VMEM((n + EDGE, width), bf16),
            pltpu.VMEM((groups * taps, wide), bf16),
            pltpu.VMEM((groups * taps, wide), bf16),
            pltpu.VMEM((groups * taps, wide), f32),
            pltpu.VMEM((n + EDGE, 1), jnp.int32),
            pltpu.VMEM((1, n + taps), jnp.int32),
        ],
        compiler_params=pltpu.CompilerParams(vmem_limit_bytes=58 * 1024 * 1024),
        cost_estimate=pl.CostEstimate(
            flops=8 * n * groups * taps * wide, bytes_accessed=16 * n * c, transcendentals=0
        ),
    )(lengths, frozen, low, place, cot, up, short, taps_f, taps_b, skip)


def by_channels(
    tokens,
    frozen,
    cotangent,
    adapter_down_weight,
    adapter_up_weight,
    short_depthwise_filter,
    long_group_filter,
    skip_direct_scale,
    document_lengths,
    window_row_position,
):
    f32, bf16 = jnp.float32, jnp.bfloat16
    rows, channels = tokens.shape
    kinds = frozen.shape[1]
    rank = adapter_down_weight.shape[0]
    shorts = short_depthwise_filter.shape[0]
    shards = lax.axis_size("ctx")
    me = lax.axis_index("ctx")
    n = rows * shards
    c = channels // shards
    taps = long_group_filter.shape[1]
    groups = long_group_filter.shape[0] // shards
    frozen_parts = frozen.reshape(rows, kinds, shards, c).transpose(2, 1, 0, 3)
    got_frozen = lax.all_to_all(frozen_parts, "ctx", split_axis=0, concat_axis=0, tiled=True)
    cot_parts = cotangent.reshape(rows, shards, c).transpose(1, 0, 2)
    got_cot = lax.all_to_all(cot_parts, "ctx", split_axis=0, concat_axis=0, tiled=True)
    part = fdot(adapter_down_weight, tokens, ((1,), (1,)))
    low_own = lax.psum(part, "tp").astype(bf16)
    place = lax.all_gather(window_row_position, "ctx", axis=0, tiled=True)
    low = lax.all_gather(low_own, "ctx", axis=0, tiled=False)
    low = low.transpose(0, 2, 1).reshape(n, rank)
    low = jnp.pad(low, ((0, 0), (0, LANES - rank)))

    def own(array):
        return lax.dynamic_slice_in_dim(array, me * c, c, array.ndim - 1)

    up = jnp.pad(own(adapter_up_weight).reshape(rank, kinds * c), ((0, LANES - rank), (0, 0)))
    short = own(short_depthwise_filter).reshape(shorts, kinds * c).astype(f32)
    skip = own(skip_direct_scale)[None, :]
    bank = lax.dynamic_slice_in_dim(long_group_filter, me * groups, groups, 0).astype(f32)
    taps_f = jnp.pad(bank[:, ::-1], ((0, 0), (1, taps - 1)))
    taps_b = jnp.pad(bank, ((0, 0), (0, taps)))
    out, up_grad, short_grad, long_line, skip_grad, back_low = core(
        document_lengths,
        got_frozen,
        low,
        place[None, :],
        got_cot.reshape(n, c),
        up,
        short,
        taps_f,
        taps_b,
        skip,
        rank,
    )
    back_low = lax.psum(back_low, ("ctx", "tp")).astype(bf16)
    out_parts = lax.all_to_all(
        out.reshape(shards, rows, c), "ctx", split_axis=0, concat_axis=0, tiled=True
    )
    mixer_out = out_parts.transpose(1, 0, 2).reshape(rows, channels)
    hot = (
        jnp.arange(n, dtype=jnp.int32)[:, None] == window_row_position[None, :]
    ).astype(bf16)
    back_own = fdot(back_low, hot).astype(bf16)
    grad_down = lax.psum(fdot(back_own, tokens), "ctx")
    long_grad = long_line[:, 1 : taps + 1][:, ::-1]
    packed = jnp.concatenate(
        [up_grad.reshape(-1), short_grad.reshape(-1), long_grad.reshape(-1), skip_grad.reshape(-1)]
    )
    packed = lax.all_gather(packed, "ctx", axis=0, tiled=False)
    cuts = [rank * kinds * c, shorts * kinds * c, groups * taps, c]
    edges = [sum(cuts[:i]) for i in range(5)]
    pieces = [packed[:, edges[i] : edges[i + 1]] for i in range(4)]

    def spread(piece, lead):
        return piece.reshape((shards,) + lead + (c,)).transpose(1, 2, 0, 3).reshape(lead + (channels,))

    return (
        mixer_out,
        grad_down,
        spread(pieces[0], (rank, kinds)),
        spread(pieces[1], (shorts, kinds)),
        pieces[2].reshape(shards * groups, taps),
        pieces[3].reshape(channels),
    )


def from_behind(value, axis, steps):
    count = lax.axis_size(axis)
    first, last = (max(0, -steps), min(count, count - steps))
    return lax.ppermute(value, axis, [(source, source + steps) for source in range(first, last)])


def doc_offsets(positions, document_lengths):
    doc_ends = jnp.cumsum(document_lengths)
    starts = doc_ends - document_lengths
    clipped = jnp.maximum(positions, 0)
    begins = jnp.max(jnp.where(starts[None, :] <= clipped[:, None], starts[None, :], 0), axis=1)
    return clipped - begins


def tap_mask(offsets, shift_tap, ndim):
    return (shift_tap <= offsets).astype(jnp.float32).reshape((-1,) + (1,) * (ndim - 1))


def pick_rows(source, row_index):
    padded = jnp.concatenate([source, jnp.zeros((1,) + source.shape[1:], source.dtype)])
    return jnp.take(padded, row_index, axis=0)


def short_apply(extended, filter_taps, offsets):
    length = offsets.shape[0]
    taps = filter_taps.shape[0]
    reach = taps - 1
    running = jnp.zeros((length,) + extended.shape[1:], jnp.float32)
    for shift_tap in range(taps):
        shifted = extended[reach - shift_tap : reach - shift_tap + length].astype(jnp.float32)
        running = running + filter_taps[shift_tap].astype(jnp.float32) * shifted * tap_mask(
            offsets, shift_tap, extended.ndim
        )
    return running


def short_back(back_ext, filter_taps, offsets_ext):
    taps = filter_taps.shape[0]
    length = back_ext.shape[0] - (taps - 1)
    running = jnp.zeros((length,) + back_ext.shape[1:], jnp.float32)
    for shift_tap in range(taps):
        shifted = back_ext[shift_tap : shift_tap + length].astype(jnp.float32)
        masked = shifted * tap_mask(
            offsets_ext[shift_tap : shift_tap + length], shift_tap, back_ext.ndim
        )
        running = running + filter_taps[shift_tap].astype(jnp.float32) * masked
    return running


def short_grad(back_post, pre_ext, offsets, taps):
    length = offsets.shape[0]
    reach = taps - 1
    back_float = back_post.astype(jnp.float32)
    collected = []
    for shift_tap in range(taps):
        shifted = pre_ext[reach - shift_tap : reach - shift_tap + length].astype(jnp.float32)
        collected.append(
            jnp.sum(back_float * shifted * tap_mask(offsets, shift_tap, pre_ext.ndim), axis=0)
        )
    return jnp.stack(collected)


def toeplitz(filter_bank):
    groups = filter_bank.shape[0]
    row_vals = jnp.concatenate(
        [
            jnp.zeros((groups, 1), filter_bank.dtype),
            filter_bank[:, ::-1],
            jnp.zeros((groups, 128), filter_bank.dtype),
        ],
        axis=1,
    )
    tiled = jnp.broadcast_to(row_vals[:, None, :], (groups, 128, 257)).reshape(groups, 128 * 257)
    return tiled[:, : 128 * 256].reshape(groups, 128, 256)


def masked_bank(filter_bank, block_off):
    row_ids = jnp.arange(128, dtype=jnp.int32)[:, None]
    col_ids = jnp.arange(256, dtype=jnp.int32)[None, :]
    allowed = (row_ids + 128 - col_ids <= block_off[:, None]).astype(filter_bank.dtype)
    return filter_bank * allowed[None]


def adapter_hidden(row_tile_block, adapter_down_weight):
    partial_low = lax.dot_general(
        adapter_down_weight,
        row_tile_block,
        (((1,), (1,)), ((), ())),
        preferred_element_type=jnp.float32,
    )
    return lax.psum(partial_low, "tp").astype(jnp.bfloat16)


def on_device(
    tokens,
    frozen,
    cotangent,
    adapter_down_weight,
    adapter_up_weight,
    short_depthwise_filter,
    long_group_filter,
    skip_direct_scale,
    document_lengths,
    window_row_position,
):
    local_rows, channels = tokens.shape
    short_count = short_depthwise_filter.shape[0]
    reach = short_count - 1
    groups = channels // 16
    blocks = local_rows // 128
    shards = lax.axis_size("ctx")
    capacity = 2 * local_rows // shards
    my_index = lax.axis_index("ctx")
    first_pos = my_index * local_rows
    all_pos = lax.all_gather(window_row_position, "ctx", axis=0, tiled=True)
    shard_ids = jnp.arange(shards, dtype=jnp.int32)
    own_dest = window_row_position // local_rows
    own_hits = (own_dest[:, None] == shard_ids[None, :]).astype(jnp.int32)
    own_rank = jnp.sum(jnp.cumsum(own_hits, axis=0) * own_hits, axis=1) - 1
    own_slot = own_dest * capacity + own_rank
    send_rows = (
        jnp.full((shards * capacity,), local_rows, jnp.int32)
        .at[own_slot]
        .set(jnp.arange(local_rows, dtype=jnp.int32))
    )
    grid_pos = all_pos.reshape(shards, local_rows)
    arriving = grid_pos // local_rows == my_index
    arrive_rank = jnp.cumsum(arriving.astype(jnp.int32), axis=1) - 1
    arrive_slot = shard_ids[:, None] * capacity + arrive_rank
    local_target = jnp.where(arriving, grid_pos % local_rows, local_rows)
    recv_rows = (
        jnp.zeros((local_rows,), jnp.int32)
        .at[local_target.reshape(-1)]
        .set(arrive_slot.reshape(-1), mode="drop")
    )
    frozen_buf = pick_rows(frozen, send_rows).reshape((shards, capacity) + frozen.shape[1:])
    token_buf = pick_rows(tokens, send_rows).reshape(shards, capacity, channels)
    got_tokens, got_frozen = (
        lax.all_to_all(token_buf, "ctx", split_axis=0, concat_axis=0, tiled=True),
        lax.all_to_all(frozen_buf, "ctx", split_axis=0, concat_axis=0, tiled=True),
    )
    packed_token_rows = jnp.take(got_tokens.reshape(shards * capacity, channels), recv_rows, axis=0)
    packed_frozen = jnp.take(
        got_frozen.reshape((shards * capacity,) + frozen.shape[1:]), recv_rows, axis=0
    )
    lowrank_product = adapter_hidden(packed_token_rows, adapter_down_weight)
    before_convolution = (
        packed_frozen.astype(jnp.float32)
        + jnp.einsum(
            "ed,ejg->djg", lowrank_product, adapter_up_weight, preferred_element_type=jnp.float32
        )
    ).astype(jnp.bfloat16)
    positions = first_pos - 127 + jnp.arange(local_rows + 255, dtype=jnp.int32)
    offsets_all = doc_offsets(positions, document_lengths)
    own_off = offsets_all[127 : 127 + local_rows]
    pre_edge = from_behind(before_convolution[-reach:], "ctx", 1)
    pre_ext = jnp.concatenate([pre_edge, before_convolution])
    post_conv = short_apply(pre_ext, short_depthwise_filter, own_off).astype(jnp.bfloat16)
    product = (post_conv[:, 1].astype(jnp.float32) * post_conv[:, 2].astype(jnp.float32)).astype(
        jnp.bfloat16
    )
    product_edge = from_behind(product[-127:], "ctx", 1)
    product_ext = jnp.concatenate([jnp.zeros((1, channels), jnp.bfloat16), product_edge, product])
    filter_bank = toeplitz(long_group_filter)
    windows = jnp.concatenate(
        [
            product_ext[:-128].reshape(blocks, 128, channels),
            product_ext[128:].reshape(blocks, 128, channels),
        ],
        axis=1,
    )
    block_offsets = own_off.reshape(blocks, 128)

    def forward_block(pieces):
        window_rows, block_off = pieces
        masked = masked_bank(filter_bank, block_off)
        return jnp.einsum(
            "gij,jgc->igc",
            masked,
            window_rows.reshape(256, groups, 16),
            preferred_element_type=jnp.float32,
        ).reshape(128, channels)

    convolved = lax.map(forward_block, (windows, block_offsets)).reshape(local_rows, channels)
    query_rows = post_conv[:, 0].astype(jnp.float32)
    key_rows = post_conv[:, 1].astype(jnp.float32)
    value_rows = post_conv[:, 2].astype(jnp.float32)
    product_float = product.astype(jnp.float32)
    direct_term = convolved + skip_direct_scale[None, :] * product_float
    mixer_out = (query_rows * direct_term).astype(jnp.bfloat16)
    grad_float = cotangent.astype(jnp.float32)
    gated_back = grad_float * query_rows
    back_conv = gated_back.astype(jnp.bfloat16)
    conv_edge = from_behind(back_conv[:127], "ctx", -1)
    edge_block = jnp.concatenate([conv_edge, jnp.zeros((1, channels), jnp.bfloat16)])

    def backward_block(pieces):
        window_rows, conv_rows, block_off = pieces
        masked = masked_bank(filter_bank, block_off)
        split_conv = conv_rows.reshape(128, groups, 16)
        spread = jnp.einsum(
            "gij,igc->jgc", masked, split_conv, preferred_element_type=jnp.float32
        ).reshape(256, channels)
        pair_sums = jnp.einsum(
            "igc,jgc->gij",
            split_conv,
            window_rows.reshape(256, groups, 16),
            preferred_element_type=jnp.float32,
        )
        skewed = jnp.pad(pair_sums.reshape(groups, 128 * 256), ((0, 0), (0, 128))).reshape(
            groups, 128, 257
        )[:, :, 1:129][:, :, ::-1]
        allowed = (jnp.arange(128, dtype=jnp.int32)[None, :] <= block_off[:, None]).astype(
            jnp.float32
        )
        return (spread, jnp.sum(skewed * allowed[None], axis=1))

    spread_all, filter_parts = lax.map(
        backward_block, (windows, back_conv.reshape(blocks, 128, channels), block_offsets)
    )
    edge_off = offsets_all[127 + local_rows : 127 + local_rows + 128]
    edge_bank = masked_bank(filter_bank, edge_off)[:, :, :128]
    edge_spread = jnp.einsum(
        "gij,igc->jgc",
        edge_bank,
        edge_block.reshape(128, groups, 16),
        preferred_element_type=jnp.float32,
    ).reshape(128, channels)
    following = jnp.concatenate([spread_all[1:, :128], edge_spread[None]], axis=0).reshape(
        local_rows, channels
    )
    product_back = (
        spread_all[:, 128:].reshape(local_rows, channels)
        + following
        + skip_direct_scale[None, :] * gated_back
    )
    grad_long = jnp.sum(filter_parts, axis=0)
    grad_skip = jnp.sum(gated_back * product_float, axis=0)
    query_back = grad_float * direct_term
    back_post = jnp.stack(
        [query_back, product_back * value_rows, product_back * key_rows], axis=1
    ).astype(jnp.bfloat16)
    post_edge = from_behind(back_post[:reach], "ctx", -1)
    back_ext = jnp.concatenate([back_post, post_edge])
    gradient_before_filter = short_back(
        back_ext, short_depthwise_filter, offsets_all[127 : 127 + local_rows + reach]
    ).astype(jnp.bfloat16)
    grad_short = short_grad(back_post, pre_ext, own_off, short_count)
    up_gradient = jnp.einsum(
        "kp,pme->kme", lowrank_product, gradient_before_filter, preferred_element_type=jnp.float32
    )
    partial_gradient = jnp.einsum(
        "ldx,idx->li", adapter_up_weight, gradient_before_filter, preferred_element_type=jnp.float32
    )
    back_low = lax.psum(partial_gradient, "tp").astype(jnp.bfloat16)
    grad_down = jnp.dot(back_low, packed_token_rows, preferred_element_type=jnp.float32)
    summed = lax.psum((grad_down, up_gradient, grad_short, grad_long, grad_skip), "ctx")
    return (mixer_out,) + tuple(summed)


def solution(mesh):
    placed = (
        P("ctx", "tp"),
        P("ctx", None, "tp"),
        P("ctx", "tp"),
        P(None, "tp"),
        P(None, None, "tp"),
        P(None, None, "tp"),
        P("tp", None),
        P("tp"),
        P(),
        P("ctx"),
    )
    channels_each = mesh.shape["ctx"] * LANES

    def run(*args):
        fits = args[0].shape[1] % channels_each == 0
        return (by_channels if fits else on_device)(*args)

    return jax.shard_map(
        run,
        mesh=mesh,
        in_specs=placed,
        out_specs=(
            P("ctx", "tp"),
            P(None, "tp"),
            P(None, None, "tp"),
            P(None, None, "tp"),
            P("tp", None),
            P("tp"),
        ),
        check_vma=False,
    )
```

```python
import functools

import jax
import jax.numpy as jnp
from jax import lax
from jax.experimental import pallas as pl
from jax.experimental.pallas import tpu as pltpu
from jax.sharding import PartitionSpec as P

EDGE = 16
LANES = 128


def fdot(left, right, contract=((1,), (0,))):
    return lax.dot_general(left, right, (contract, ((), ())), preferred_element_type=jnp.float32)


def doc_starts(pos, lengths_ref):
    begins = jnp.zeros_like(pos)
    running = jnp.int32(0)
    for doc in range(lengths_ref.shape[0]):
        begins = jnp.where(pos >= running, running, begins)
        running = running + lengths_ref[doc]
    return begins


def ctx_peers():
    me, count = lax.axis_index("ctx"), lax.axis_size("ctx")
    return me, [(d, lax.rem(me + d, count)) for d in range(1, count)]


def tp_peers():
    me, count = lax.axis_index("tp"), lax.axis_size("tp")
    return me, [(d, lax.rem(me + d, count)) for d in range(1, count)]


def greet():
    barrier = pltpu.get_barrier_semaphore()
    waits = 0
    for axis, (_, peers) in (("ctx", ctx_peers()), ("tp", tp_peers())):
        for _, peer in peers:
            pl.semaphore_signal(
                barrier, inc=1, device_id={axis: peer}, device_id_type=pl.DeviceIdType.MESH
            )
            waits += 1
    pl.semaphore_wait(barrier, waits)


def push(src, dst, send_sem, recv_sem, axis, peer):
    copy = pltpu.make_async_remote_copy(
        src_ref=src,
        dst_ref=dst,
        send_sem=send_sem,
        recv_sem=recv_sem,
        device_id={axis: peer},
        device_id_type=pl.DeviceIdType.MESH,
    )
    copy.start()
    return copy


def part_of(index, size):
    return pl.ds(pl.multiple_of(index * size, size), size)


def mixer_kernel(
    lengths_ref,
    frozen_ref,
    cot_in_ref,
    tokens_ref,
    down_ref,
    pos_ref,
    up_ref,
    short_ref,
    taps_f_ref,
    taps_b_ref,
    skip_ref,
    mixer_out,
    grad_down,
    grad_up,
    grad_small,
    grad_long,
    got_frozen,
    cot_ref,
    low_all,
    place_all,
    out_ref,
    up_grad_ref,
    short_grad_ref,
    long_grad_ref,
    back_low_ref,
    low_got,
    back_parts,
    back_own_low,
    back_all,
    down_part,
    down_got,
    down_own,
    low_parts,
    low_own,
    rhs,
    pre,
    low_win,
    post,
    prod,
    back,
    back_post,
    bank_f,
    bank_b,
    pair_acc,
    start_col,
    start_row,
    send_sems,
    recv_sems,
    own_sems,
    tp_send,
    tp_recv,
):
    n, c = cot_ref.shape
    groups, wide = taps_f_ref.shape
    taps = wide // 2
    per = c // groups
    shards, kinds, rows, _ = got_frozen.shape
    width = kinds * c
    blocks = n // taps
    shorts = short_ref.shape[0]
    rank = down_ref.shape[0]
    f32, bf16 = jnp.float32, jnp.bfloat16
    me, peers = ctx_peers()
    tp_me, tp_others = tp_peers()
    mine, my_rows = part_of(me, c), part_of(me, rows)
    greet()

    def everyone(step, source, target):
        return [
            push(source(peer), target, send_sems.at[step, d], recv_sems.at[step, d], "ctx", peer)
            for d, peer in peers
        ]

    def tp_swap(step, parts):
        return [
            push(
                parts.at[tp_me],
                parts.at[tp_me],
                tp_send.at[step, d],
                tp_recv.at[step, d],
                "tp",
                peer,
            )
            for d, peer in tp_others
        ]

    def finish(copies):
        for copy in copies:
            copy.wait()

    def tidy(parts, count):
        total = parts[0]
        for t in range(1, count):
            total = total + parts[t]
        return total

    places = everyone(8, lambda peer: pos_ref, place_all.at[me])
    frozens = everyone(
        9, lambda peer: frozen_ref.at[:, :, part_of(peer, c)], got_frozen.at[me]
    )
    own_frozen = pltpu.make_async_copy(frozen_ref.at[:, :, mine], got_frozen.at[me], own_sems.at[0])
    own_frozen.start()
    own_cot = pltpu.make_async_copy(cot_in_ref.at[:, mine], cot_ref.at[my_rows], own_sems.at[1])
    own_cot.start()
    place_all[me] = pos_ref[...]
    low_parts[tp_me] = fdot(down_ref[...], tokens_ref[...], ((1,), (1,)))
    swaps = tp_swap(0, low_parts)
    cots = everyone(10, lambda peer: cot_in_ref.at[:, part_of(peer, c)], cot_ref.at[my_rows])
    finish(swaps)
    low_own[...] = tidy(low_parts, low_parts.shape[0]).astype(bf16)
    low_all[me] = low_own[...]
    lows = everyone(11, lambda peer: low_own, low_all.at[me])

    start_col[...] = doc_starts(
        lax.broadcasted_iota(jnp.int32, start_col.shape, 0), lengths_ref
    )
    start_row[...] = doc_starts(
        lax.broadcasted_iota(jnp.int32, start_row.shape, 1), lengths_ref
    )

    for g in range(groups):
        span = slice(g * taps, (g + 1) * taps)
        for taps_ref, bank in ((taps_f_ref, bank_f), (taps_b_ref, bank_b)):
            line = jnp.broadcast_to(taps_ref[g : g + 1, :], (taps, wide))
            bank[span, :] = pltpu.roll(line, 0, 1, stride=1, stride_axis=0).astype(bf16)

    unit = jnp.where(
        lax.broadcasted_iota(jnp.int32, (rank, LANES), 0)
        == lax.broadcasted_iota(jnp.int32, (rank, LANES), 1),
        1.0,
        0.0,
    ).astype(bf16)

    finish(places)
    finish(lows)
    for d in range(shards):
        if d == 0:
            own_frozen.wait()
        else:
            frozens[d - 1].wait()
        j = lax.rem(me + shards - d, shards)
        at = part_of(j, rows)
        low = fdot(low_all[j], unit, ((0,), (0,))).astype(bf16)
        for a in range(kinds):
            cols = slice(a * c, (a + 1) * c)
            rhs[at, cols] = (got_frozen[j, a].astype(f32) + fdot(low, up_ref[:, cols])).astype(bf16)
        rhs[at, width:] = low

    pre[:EDGE, :] = jnp.zeros((EDGE, width), bf16)
    tall = rows * 2

    @pl.loop(0, n // tall)
    def _(w):
        base = pl.multiple_of(w * tall, tall)
        spot = lax.broadcasted_iota(jnp.int32, (tall, rows), 0) + base
        hot = jnp.concatenate(
            [jnp.where(place_all[j] == spot, 1.0, 0.0).astype(bf16) for j in range(shards)], axis=1
        )
        moved = fdot(hot, rhs[...]).astype(bf16)
        pre[pl.ds(pl.multiple_of(base + EDGE, EDGE), tall), :] = moved[:, :width]
        low_win[pl.ds(base, tall), :] = moved[:, width:]

    own_cot.wait()
    finish(cots)
    prod[:taps, :] = jnp.zeros((taps, c), bf16)
    back[n:, :] = jnp.zeros((taps, c), bf16)

    @pl.loop(0, blocks)
    def _(b):
        base = pl.multiple_of(b * taps, taps)
        at = pl.ds(base, taps)
        ext = pre[pl.ds(base, taps + EDGE), :].astype(f32)
        off = lax.broadcasted_iota(jnp.int32, (taps, 1), 0) + base - start_col[at, :]
        total = jnp.zeros((taps, width), f32)
        for s in range(shorts):
            gate = (off >= s).astype(f32)
            total = total + short_ref[s : s + 1, :] * ext[EDGE - s : EDGE - s + taps] * gate
        rounded = total.astype(bf16)
        post[at, :] = rounded
        rounded = rounded.astype(f32)
        prod[pl.ds(pl.multiple_of(base + taps, taps), taps), :] = (
            rounded[:, c : 2 * c] * rounded[:, 2 * c :]
        ).astype(bf16)
        back[at, :] = (cot_ref[at, :].astype(f32) * rounded[:, :c]).astype(bf16)

    pair_acc[...] = jnp.zeros_like(pair_acc)
    short_grad_ref[...] = jnp.zeros_like(short_grad_ref)
    back_post[n:, :] = jnp.zeros((EDGE, width), bf16)
    lane_group = lax.broadcasted_iota(jnp.int32, (taps, c), 1) // per

    turned = wide - 1 - lax.broadcasted_iota(jnp.int32, (taps, wide), 1)
    flip = jnp.where(
        lax.broadcasted_iota(jnp.int32, (wide, wide), 0)
        + lax.broadcasted_iota(jnp.int32, (wide, wide), 1)
        == wide - 1,
        1.0,
        0.0,
    ).astype(bf16)

    def pick(stacked):
        chosen = stacked[:taps]
        for g in range(1, groups):
            chosen = jnp.where(lane_group == g, stacked[g * taps : (g + 1) * taps], chosen)
        return chosen

    @pl.loop(0, blocks)
    def _(b):
        base = pl.multiple_of(b * taps, taps)
        at = pl.ds(base, taps)
        window = prod[pl.ds(base, 2 * taps), :]
        ahead = back[pl.ds(base, 2 * taps), :]
        col_pos = lax.broadcasted_iota(jnp.int32, (taps, wide), 1) + (base - taps)
        same_f = col_pos >= start_col[at, :]
        gate_f = jnp.where(same_f, 1.0, 0.0).astype(bf16)
        gate_r = jnp.where(turned + (base - taps) >= start_col[at, :], 1.0, 0.0)
        row_pos = lax.broadcasted_iota(jnp.int32, (taps, wide), 0) + base
        same_b = row_pos >= start_row[:, pl.ds(base, wide)]
        gate_b = jnp.where(same_b, 1.0, 0.0).astype(bf16)
        many_f = jnp.concatenate([gate_f] * groups, axis=0)
        many_b = jnp.concatenate([gate_b] * groups, axis=0)
        conv = pick(fdot(bank_f[...] * many_f, window))
        spread = pick(fdot(bank_b[...] * many_b, ahead))
        here = ahead[:taps]
        split = jnp.concatenate(
            [jnp.where(lane_group == g, here, jnp.zeros_like(here)) for g in range(groups)], axis=0
        )
        pairs = fdot(split, fdot(flip, window).astype(bf16), ((1,), (1,)))
        for g in range(groups):
            span = slice(g * taps, (g + 1) * taps)
            pair_acc[span, :] += pairs[span] * gate_r
        product = window[taps:].astype(f32)
        cot = cot_ref[at, :].astype(f32)
        query = post[at, :c].astype(f32)
        key = post[at, c : 2 * c].astype(f32)
        value = post[at, 2 * c :].astype(f32)
        gated = cot * query
        skip = skip_ref[...]
        direct = conv + skip * product
        out_ref[at, :] = (query * direct).astype(bf16)
        product_back = spread + skip * gated
        short_grad_ref[shorts : shorts + 1, :c] += jnp.sum(gated * product, axis=0, keepdims=True)
        back_post[at, :c] = (cot * direct).astype(bf16)
        back_post[at, c : 2 * c] = (product_back * value).astype(bf16)
        back_post[at, 2 * c :] = (product_back * key).astype(bf16)

    copies = everyone(1, lambda peer: out_ref.at[part_of(peer, rows)], mixer_out.at[:, mine])
    own = [pltpu.make_async_copy(out_ref.at[my_rows], mixer_out.at[:, mine], own_sems.at[0])]
    own[0].start()
    for g in range(groups):
        span = slice(g * taps, (g + 1) * taps)
        square = pltpu.roll(pair_acc[span, :], wide - taps + 1, 1, stride=1, stride_axis=0)
        long_grad_ref[g : g + 1, :] = jnp.sum(square[:, :taps], axis=0, keepdims=True)

    @pl.loop(0, blocks)
    def _(b):
        base = pl.multiple_of(b * taps, taps)
        at = pl.ds(base, taps)
        ext = pre[pl.ds(base, taps + EDGE), :].astype(f32)
        back_ext = back_post[pl.ds(base, taps + EDGE), :].astype(f32)
        off = (
            lax.broadcasted_iota(jnp.int32, (taps + EDGE, 1), 0)
            + base
            - start_col[pl.ds(base, taps + EDGE), :]
        )
        total = jnp.zeros((taps, width), f32)
        for s in range(shorts):
            masked = back_ext * (off >= s).astype(f32)
            total = total + short_ref[s : s + 1, :] * masked[s : s + taps]
            short_grad_ref[s : s + 1, :] += jnp.sum(
                masked[:taps] * ext[EDGE - s : EDGE - s + taps], axis=0, keepdims=True
            )
        rhs[at, :width] = total.astype(bf16)

    back_pre = rhs[:, :width]
    up_grad = fdot(low_win[...], back_pre, ((0,), (0,)))
    for a in range(kinds):
        up_grad_ref[a] = up_grad[:rank, a * c : (a + 1) * c]
    back_low_ref[...] = fdot(up_ref[:rank, :], back_pre, ((1,), (1,)))
    reduce_low = everyone(0, lambda peer: back_low_ref.at[:, part_of(peer, rows)], low_got.at[me])
    low_got[me] = back_low_ref[:, my_rows]
    copies += everyone(2, lambda peer: up_grad_ref, grad_up.at[:, :, mine])
    copies += everyone(3, lambda peer: short_grad_ref, grad_small.at[me])
    copies += everyone(4, lambda peer: long_grad_ref, grad_long.at[part_of(me, groups)])
    own += [
        pltpu.make_async_copy(up_grad_ref, grad_up.at[:, :, mine], own_sems.at[1]),
        pltpu.make_async_copy(short_grad_ref, grad_small.at[me], own_sems.at[2]),
        pltpu.make_async_copy(long_grad_ref, grad_long.at[part_of(me, groups)], own_sems.at[3]),
    ]
    for copy in own[1:]:
        copy.start()
    finish(reduce_low)
    total = low_got[0]
    for j in range(1, shards):
        total = total + low_got[j]
    back_parts[tp_me] = total
    finish(tp_swap(1, back_parts))
    total = back_parts[0]
    for t in range(1, back_parts.shape[0]):
        total = total + back_parts[t]
    back_own_low[...] = total.astype(bf16)
    spread = everyone(5, lambda peer: back_own_low, back_all.at[me])
    back_all[me] = total.astype(bf16)
    finish(spread)
    back_own = jnp.zeros((rank, rows), jnp.float32)
    for j in range(shards):
        spot = lax.broadcasted_iota(jnp.int32, (rows, rows), 0) + j * rows
        hot = jnp.where(pos_ref[...] == spot, 1.0, 0.0).astype(bf16)
        back_own = back_own + fdot(back_all[j], hot)
    down_part[...] = fdot(back_own.astype(bf16), tokens_ref[...])
    reduce_down = everyone(6, lambda peer: down_part.at[:, part_of(peer, c)], down_got.at[me])
    down_got[me] = down_part[:, mine]
    finish(reduce_down)
    total = down_got[0]
    for j in range(1, shards):
        total = total + down_got[j]
    down_own[...] = total
    copies += everyone(7, lambda peer: down_own, grad_down.at[:, mine])
    last = pltpu.make_async_copy(down_own, grad_down.at[:, mine], own_sems.at[4])
    last.start()
    finish(copies + own + [last])


def mixer(lengths, frozen, cot, tokens, down, pos, up, short, taps_f, taps_b, skip):
    kinds, rows, channels = frozen.shape
    shards, tps = lax.axis_size("ctx"), lax.axis_size("tp")
    n, c = rows * shards, channels // shards
    groups, wide = taps_f.shape
    taps = wide // 2
    width = kinds * c
    rank = down.shape[0]
    small = -(-(short.shape[0] + 1) // 8) * 8
    f32, bf16, i32 = jnp.float32, jnp.bfloat16, jnp.int32
    shape = jax.ShapeDtypeStruct
    vmem, hbm = pl.BlockSpec(memory_space=pltpu.VMEM), pl.BlockSpec(memory_space=pl.ANY)
    return pl.pallas_call(
        mixer_kernel,
        out_shape=(
            shape((rows, channels), bf16),
            shape((rank, channels), f32),
            shape((kinds, rank, channels), f32),
            shape((shards, small, width), f32),
            shape((shards * groups, taps), f32),
        ),
        in_specs=[pl.BlockSpec(memory_space=pltpu.SMEM), hbm, hbm] + [vmem] * 8,
        out_specs=(hbm,) * 5,
        scratch_shapes=[
            pltpu.VMEM((shards, kinds, rows, c), bf16),
            pltpu.VMEM((n, c), bf16),
            pltpu.VMEM((shards, rank, rows), bf16),
            pltpu.VMEM((shards, 1, rows), i32),
            pltpu.VMEM((n, c), bf16),
            pltpu.VMEM((kinds, rank, c), f32),
            pltpu.VMEM((small, width), f32),
            pltpu.VMEM((groups, taps), f32),
            pltpu.VMEM((rank, n), f32),
            pltpu.VMEM((shards, rank, rows), f32),
            pltpu.VMEM((tps, rank, rows), f32),
            pltpu.VMEM((rank, rows), bf16),
            pltpu.VMEM((shards, rank, rows), bf16),
            pltpu.VMEM((rank, channels), f32),
            pltpu.VMEM((shards, rank, c), f32),
            pltpu.VMEM((rank, c), f32),
            pltpu.VMEM((tps, rank, rows), f32),
            pltpu.VMEM((rank, rows), bf16),
            pltpu.VMEM((n, width + LANES), bf16),
            pltpu.VMEM((n + EDGE, width), bf16),
            pltpu.VMEM((n, LANES), bf16),
            pltpu.VMEM((n, width), bf16),
            pltpu.VMEM((n + taps, c), bf16),
            pltpu.VMEM((n + taps, c), bf16),
            pltpu.VMEM((n + EDGE, width), bf16),
            pltpu.VMEM((groups * taps, wide), bf16),
            pltpu.VMEM((groups * taps, wide), bf16),
            pltpu.VMEM((groups * taps, wide), f32),
            pltpu.VMEM((n + EDGE, 1), i32),
            pltpu.VMEM((1, n + taps), i32),
            pltpu.SemaphoreType.DMA((12, shards)),
            pltpu.SemaphoreType.DMA((12, shards)),
            pltpu.SemaphoreType.DMA((5,)),
            pltpu.SemaphoreType.DMA((2, tps)),
            pltpu.SemaphoreType.DMA((2, tps)),
        ],
        compiler_params=pltpu.CompilerParams(
            collective_id=0, has_side_effects=True, vmem_limit_bytes=58 * 1024 * 1024
        ),
        cost_estimate=pl.CostEstimate(
            flops=8 * n * groups * taps * wide, bytes_accessed=16 * n * c, transcendentals=0
        ),
    )(lengths, frozen, cot, tokens, down, pos, up, short, taps_f, taps_b, skip)


def by_channels(
    tokens,
    frozen,
    cotangent,
    adapter_down_weight,
    adapter_up_weight,
    short_depthwise_filter,
    long_group_filter,
    skip_direct_scale,
    document_lengths,
    window_row_position,
):
    f32, bf16 = jnp.float32, jnp.bfloat16
    rows, channels = tokens.shape
    kinds = frozen.shape[1]
    rank = adapter_down_weight.shape[0]
    shorts = short_depthwise_filter.shape[0]
    shards = lax.axis_size("ctx")
    me = lax.axis_index("ctx")
    n = rows * shards
    c = channels // shards
    taps = long_group_filter.shape[1]
    groups = long_group_filter.shape[0] // shards
    pos = window_row_position[None, :]
    def own(array):
        return lax.dynamic_slice_in_dim(array, me * c, c, array.ndim - 1)

    up = jnp.pad(own(adapter_up_weight).reshape(rank, kinds * c), ((0, LANES - rank), (0, 0)))
    short = own(short_depthwise_filter).reshape(shorts, kinds * c).astype(f32)
    skip = own(skip_direct_scale)[None, :]
    bank = lax.dynamic_slice_in_dim(long_group_filter, me * groups, groups, 0).astype(f32)
    taps_f = jnp.pad(bank[:, ::-1], ((0, 0), (1, taps - 1)))
    taps_b = jnp.pad(bank, ((0, 0), (0, taps)))
    mixer_out, grad_down, grad_up, grad_small, grad_long = mixer(
        document_lengths,
        frozen.transpose(1, 0, 2),
        cotangent,
        tokens,
        adapter_down_weight,
        pos,
        up,
        short,
        taps_f,
        taps_b,
        skip,
    )
    grad_short = grad_small[:, :shorts].reshape(shards, shorts, kinds, c).transpose(1, 2, 0, 3)
    return (
        mixer_out,
        grad_down,
        grad_up.transpose(1, 0, 2),
        grad_short.reshape(shorts, kinds, channels),
        grad_long,
        grad_small[:, shorts, :c].reshape(channels),
    )


def from_behind(value, axis, steps):
    count = lax.axis_size(axis)
    first, last = (max(0, -steps), min(count, count - steps))
    return lax.ppermute(value, axis, [(source, source + steps) for source in range(first, last)])


def doc_offsets(positions, document_lengths):
    doc_ends = jnp.cumsum(document_lengths)
    starts = doc_ends - document_lengths
    clipped = jnp.maximum(positions, 0)
    begins = jnp.max(jnp.where(starts[None, :] <= clipped[:, None], starts[None, :], 0), axis=1)
    return clipped - begins


def tap_mask(offsets, shift_tap, ndim):
    return (shift_tap <= offsets).astype(jnp.float32).reshape((-1,) + (1,) * (ndim - 1))


def pick_rows(source, row_index):
    padded = jnp.concatenate([source, jnp.zeros((1,) + source.shape[1:], source.dtype)])
    return jnp.take(padded, row_index, axis=0)


def short_apply(extended, filter_taps, offsets):
    length = offsets.shape[0]
    taps = filter_taps.shape[0]
    reach = taps - 1
    running = jnp.zeros((length,) + extended.shape[1:], jnp.float32)
    for shift_tap in range(taps):
        shifted = extended[reach - shift_tap : reach - shift_tap + length].astype(jnp.float32)
        running = running + filter_taps[shift_tap].astype(jnp.float32) * shifted * tap_mask(
            offsets, shift_tap, extended.ndim
        )
    return running


def short_back(back_ext, filter_taps, offsets_ext):
    taps = filter_taps.shape[0]
    length = back_ext.shape[0] - (taps - 1)
    running = jnp.zeros((length,) + back_ext.shape[1:], jnp.float32)
    for shift_tap in range(taps):
        shifted = back_ext[shift_tap : shift_tap + length].astype(jnp.float32)
        masked = shifted * tap_mask(
            offsets_ext[shift_tap : shift_tap + length], shift_tap, back_ext.ndim
        )
        running = running + filter_taps[shift_tap].astype(jnp.float32) * masked
    return running


def short_grad(back_post, pre_ext, offsets, taps):
    length = offsets.shape[0]
    reach = taps - 1
    back_float = back_post.astype(jnp.float32)
    collected = []
    for shift_tap in range(taps):
        shifted = pre_ext[reach - shift_tap : reach - shift_tap + length].astype(jnp.float32)
        collected.append(
            jnp.sum(back_float * shifted * tap_mask(offsets, shift_tap, pre_ext.ndim), axis=0)
        )
    return jnp.stack(collected)


def toeplitz(filter_bank):
    groups = filter_bank.shape[0]
    row_vals = jnp.concatenate(
        [
            jnp.zeros((groups, 1), filter_bank.dtype),
            filter_bank[:, ::-1],
            jnp.zeros((groups, 128), filter_bank.dtype),
        ],
        axis=1,
    )
    tiled = jnp.broadcast_to(row_vals[:, None, :], (groups, 128, 257)).reshape(groups, 128 * 257)
    return tiled[:, : 128 * 256].reshape(groups, 128, 256)


def masked_bank(filter_bank, block_off):
    row_ids = jnp.arange(128, dtype=jnp.int32)[:, None]
    col_ids = jnp.arange(256, dtype=jnp.int32)[None, :]
    allowed = (row_ids + 128 - col_ids <= block_off[:, None]).astype(filter_bank.dtype)
    return filter_bank * allowed[None]


def adapter_hidden(row_tile_block, adapter_down_weight):
    partial_low = lax.dot_general(
        adapter_down_weight,
        row_tile_block,
        (((1,), (1,)), ((), ())),
        preferred_element_type=jnp.float32,
    )
    return lax.psum(partial_low, "tp").astype(jnp.bfloat16)


def on_device(
    tokens,
    frozen,
    cotangent,
    adapter_down_weight,
    adapter_up_weight,
    short_depthwise_filter,
    long_group_filter,
    skip_direct_scale,
    document_lengths,
    window_row_position,
):
    local_rows, channels = tokens.shape
    short_count = short_depthwise_filter.shape[0]
    reach = short_count - 1
    groups = channels // 16
    blocks = local_rows // 128
    shards = lax.axis_size("ctx")
    capacity = 2 * local_rows // shards
    my_index = lax.axis_index("ctx")
    first_pos = my_index * local_rows
    all_pos = lax.all_gather(window_row_position, "ctx", axis=0, tiled=True)
    shard_ids = jnp.arange(shards, dtype=jnp.int32)
    own_dest = window_row_position // local_rows
    own_hits = (own_dest[:, None] == shard_ids[None, :]).astype(jnp.int32)
    own_rank = jnp.sum(jnp.cumsum(own_hits, axis=0) * own_hits, axis=1) - 1
    own_slot = own_dest * capacity + own_rank
    send_rows = (
        jnp.full((shards * capacity,), local_rows, jnp.int32)
        .at[own_slot]
        .set(jnp.arange(local_rows, dtype=jnp.int32))
    )
    grid_pos = all_pos.reshape(shards, local_rows)
    arriving = grid_pos // local_rows == my_index
    arrive_rank = jnp.cumsum(arriving.astype(jnp.int32), axis=1) - 1
    arrive_slot = shard_ids[:, None] * capacity + arrive_rank
    local_target = jnp.where(arriving, grid_pos % local_rows, local_rows)
    recv_rows = (
        jnp.zeros((local_rows,), jnp.int32)
        .at[local_target.reshape(-1)]
        .set(arrive_slot.reshape(-1), mode="drop")
    )
    frozen_buf = pick_rows(frozen, send_rows).reshape((shards, capacity) + frozen.shape[1:])
    token_buf = pick_rows(tokens, send_rows).reshape(shards, capacity, channels)
    got_tokens, got_frozen = (
        lax.all_to_all(token_buf, "ctx", split_axis=0, concat_axis=0, tiled=True),
        lax.all_to_all(frozen_buf, "ctx", split_axis=0, concat_axis=0, tiled=True),
    )
    packed_token_rows = jnp.take(got_tokens.reshape(shards * capacity, channels), recv_rows, axis=0)
    packed_frozen = jnp.take(
        got_frozen.reshape((shards * capacity,) + frozen.shape[1:]), recv_rows, axis=0
    )
    lowrank_product = adapter_hidden(packed_token_rows, adapter_down_weight)
    before_convolution = (
        packed_frozen.astype(jnp.float32)
        + jnp.einsum(
            "ed,ejg->djg", lowrank_product, adapter_up_weight, preferred_element_type=jnp.float32
        )
    ).astype(jnp.bfloat16)
    positions = first_pos - 127 + jnp.arange(local_rows + 255, dtype=jnp.int32)
    offsets_all = doc_offsets(positions, document_lengths)
    own_off = offsets_all[127 : 127 + local_rows]
    pre_edge = from_behind(before_convolution[-reach:], "ctx", 1)
    pre_ext = jnp.concatenate([pre_edge, before_convolution])
    post_conv = short_apply(pre_ext, short_depthwise_filter, own_off).astype(jnp.bfloat16)
    product = (post_conv[:, 1].astype(jnp.float32) * post_conv[:, 2].astype(jnp.float32)).astype(
        jnp.bfloat16
    )
    product_edge = from_behind(product[-127:], "ctx", 1)
    product_ext = jnp.concatenate([jnp.zeros((1, channels), jnp.bfloat16), product_edge, product])
    filter_bank = toeplitz(long_group_filter)
    windows = jnp.concatenate(
        [
            product_ext[:-128].reshape(blocks, 128, channels),
            product_ext[128:].reshape(blocks, 128, channels),
        ],
        axis=1,
    )
    block_offsets = own_off.reshape(blocks, 128)

    def forward_block(pieces):
        window_rows, block_off = pieces
        masked = masked_bank(filter_bank, block_off)
        return jnp.einsum(
            "gij,jgc->igc",
            masked,
            window_rows.reshape(256, groups, 16),
            preferred_element_type=jnp.float32,
        ).reshape(128, channels)

    convolved = lax.map(forward_block, (windows, block_offsets)).reshape(local_rows, channels)
    query_rows = post_conv[:, 0].astype(jnp.float32)
    key_rows = post_conv[:, 1].astype(jnp.float32)
    value_rows = post_conv[:, 2].astype(jnp.float32)
    product_float = product.astype(jnp.float32)
    direct_term = convolved + skip_direct_scale[None, :] * product_float
    mixer_out = (query_rows * direct_term).astype(jnp.bfloat16)
    grad_float = cotangent.astype(jnp.float32)
    gated_back = grad_float * query_rows
    back_conv = gated_back.astype(jnp.bfloat16)
    conv_edge = from_behind(back_conv[:127], "ctx", -1)
    edge_block = jnp.concatenate([conv_edge, jnp.zeros((1, channels), jnp.bfloat16)])

    def backward_block(pieces):
        window_rows, conv_rows, block_off = pieces
        masked = masked_bank(filter_bank, block_off)
        split_conv = conv_rows.reshape(128, groups, 16)
        spread = jnp.einsum(
            "gij,igc->jgc", masked, split_conv, preferred_element_type=jnp.float32
        ).reshape(256, channels)
        pair_sums = jnp.einsum(
            "igc,jgc->gij",
            split_conv,
            window_rows.reshape(256, groups, 16),
            preferred_element_type=jnp.float32,
        )
        skewed = jnp.pad(pair_sums.reshape(groups, 128 * 256), ((0, 0), (0, 128))).reshape(
            groups, 128, 257
        )[:, :, 1:129][:, :, ::-1]
        allowed = (jnp.arange(128, dtype=jnp.int32)[None, :] <= block_off[:, None]).astype(
            jnp.float32
        )
        return (spread, jnp.sum(skewed * allowed[None], axis=1))

    spread_all, filter_parts = lax.map(
        backward_block, (windows, back_conv.reshape(blocks, 128, channels), block_offsets)
    )
    edge_off = offsets_all[127 + local_rows : 127 + local_rows + 128]
    edge_bank = masked_bank(filter_bank, edge_off)[:, :, :128]
    edge_spread = jnp.einsum(
        "gij,igc->jgc",
        edge_bank,
        edge_block.reshape(128, groups, 16),
        preferred_element_type=jnp.float32,
    ).reshape(128, channels)
    following = jnp.concatenate([spread_all[1:, :128], edge_spread[None]], axis=0).reshape(
        local_rows, channels
    )
    product_back = (
        spread_all[:, 128:].reshape(local_rows, channels)
        + following
        + skip_direct_scale[None, :] * gated_back
    )
    grad_long = jnp.sum(filter_parts, axis=0)
    grad_skip = jnp.sum(gated_back * product_float, axis=0)
    query_back = grad_float * direct_term
    back_post = jnp.stack(
        [query_back, product_back * value_rows, product_back * key_rows], axis=1
    ).astype(jnp.bfloat16)
    post_edge = from_behind(back_post[:reach], "ctx", -1)
    back_ext = jnp.concatenate([back_post, post_edge])
    gradient_before_filter = short_back(
        back_ext, short_depthwise_filter, offsets_all[127 : 127 + local_rows + reach]
    ).astype(jnp.bfloat16)
    grad_short = short_grad(back_post, pre_ext, own_off, short_count)
    up_gradient = jnp.einsum(
        "kp,pme->kme", lowrank_product, gradient_before_filter, preferred_element_type=jnp.float32
    )
    partial_gradient = jnp.einsum(
        "ldx,idx->li", adapter_up_weight, gradient_before_filter, preferred_element_type=jnp.float32
    )
    back_low = lax.psum(partial_gradient, "tp").astype(jnp.bfloat16)
    grad_down = jnp.dot(back_low, packed_token_rows, preferred_element_type=jnp.float32)
    summed = lax.psum((grad_down, up_gradient, grad_short, grad_long, grad_skip), "ctx")
    return (mixer_out,) + tuple(summed)


def solution(mesh):
    placed = (
        P("ctx", "tp"),
        P("ctx", None, "tp"),
        P("ctx", "tp"),
        P(None, "tp"),
        P(None, None, "tp"),
        P(None, None, "tp"),
        P("tp", None),
        P("tp"),
        P(),
        P("ctx"),
    )
    channels_each = mesh.shape["ctx"] * LANES

    def run(*args):
        fits = args[0].shape[1] % channels_each == 0
        return (by_channels if fits else on_device)(*args)

    return jax.shard_map(
        run,
        mesh=mesh,
        in_specs=placed,
        out_specs=(
            P("ctx", "tp"),
            P(None, "tp"),
            P(None, None, "tp"),
            P(None, None, "tp"),
            P("tp", None),
            P("tp"),
        ),
        check_vma=False,
    )
```

```python
import functools

import jax
import jax.numpy as jnp
from jax import lax
from jax.experimental import pallas as pl
from jax.experimental.pallas import tpu as pltpu
from jax.sharding import PartitionSpec as P

EDGE = 16
LANES = 128


def fdot(left, right, contract=((1,), (0,))):
    return lax.dot_general(left, right, (contract, ((), ())), preferred_element_type=jnp.float32)


def doc_starts(pos, lengths_ref):
    begins = jnp.zeros_like(pos)
    running = jnp.int32(0)
    for doc in range(lengths_ref.shape[0]):
        begins = jnp.where(pos >= running, running, begins)
        running = running + lengths_ref[doc]
    return begins


def ctx_peers():
    me, count = lax.axis_index("ctx"), lax.axis_size("ctx")
    return me, [(d, lax.rem(me + d, count)) for d in range(1, count)]


def tp_peers():
    me, count = lax.axis_index("tp"), lax.axis_size("tp")
    return me, [(d, lax.rem(me + d, count)) for d in range(1, count)]


def greet():
    barrier = pltpu.get_barrier_semaphore()
    waits = 0
    for axis, (_, peers) in (("ctx", ctx_peers()), ("tp", tp_peers())):
        for _, peer in peers:
            pl.semaphore_signal(
                barrier, inc=1, device_id={axis: peer}, device_id_type=pl.DeviceIdType.MESH
            )
            waits += 1
    pl.semaphore_wait(barrier, waits)


def push(src, dst, send_sem, recv_sem, axis, peer):
    copy = pltpu.make_async_remote_copy(
        src_ref=src,
        dst_ref=dst,
        send_sem=send_sem,
        recv_sem=recv_sem,
        device_id={axis: peer},
        device_id_type=pl.DeviceIdType.MESH,
    )
    copy.start()
    return copy


def part_of(index, size):
    return pl.ds(pl.multiple_of(index * size, size), size)


def mixer_kernel(
    lengths_ref,
    frozen_ref,
    cot_in_ref,
    tokens_ref,
    down_ref,
    pos_ref,
    up_ref,
    short_ref,
    filter_ref,
    skip_ref,
    mixer_out,
    grad_down,
    grad_up,
    grad_small,
    grad_long,
    got_frozen,
    got_cot,
    low_all,
    place_all,
    out_buf,
    up_own,
    small_own,
    long_own,
    back_low,
    low_got,
    back_parts,
    back_own_low,
    back_all,
    down_part,
    down_got,
    down_own,
    low_parts,
    low_own,
    hot_ref,
    rhs,
    pre,
    low_win,
    post,
    prod,
    back,
    back_post,
    taps_f,
    taps_b,
    bank_f,
    bank_b,
    pair_acc,
    start_col,
    start_row,
    send_sems,
    recv_sems,
    own_sems,
    tp_send,
    tp_recv,
):
    slabs, shards, kinds, rows, lanes = got_frozen.shape
    n, c = rows * shards, lanes * slabs
    groups, wide = taps_f.shape
    taps = wide // 2
    per = c // groups
    some = groups // slabs
    width = kinds * lanes
    blocks = n // taps
    shorts = short_ref.shape[0] // kinds
    rank = down_ref.shape[0]
    f32, bf16 = jnp.float32, jnp.bfloat16
    me, peers = ctx_peers()
    tp_me, tp_others = tp_peers()
    mine, my_rows = part_of(me, c), part_of(me, rows)
    greet()

    def everyone(step, source, target):
        return [
            push(source(peer), target, send_sems.at[step, d], recv_sems.at[step, d], "ctx", peer)
            for d, peer in peers
        ]

    def tp_swap(step, parts):
        return [
            push(
                parts.at[tp_me],
                parts.at[tp_me],
                tp_send.at[step, d],
                tp_recv.at[step, d],
                "tp",
                peer,
            )
            for d, peer in tp_others
        ]

    def keep(step, source, target):
        copy = pltpu.make_async_copy(source, target, own_sems.at[step])
        copy.start()
        return copy

    def finish(copies):
        for copy in copies:
            copy.wait()

    def tidy(parts, count):
        total = parts[0]
        for t in range(1, count):
            total = total + parts[t]
        return total

    def columns(index, h):
        return pl.ds(pl.multiple_of(index * c + h * lanes, lanes), lanes)

    def fetch(h):
        frozens = everyone(
            9 + slabs + h, lambda peer: frozen_ref.at[:, :, columns(peer, h)], got_frozen.at[h, me]
        )
        cots = everyone(
            9 + 2 * slabs + h,
            lambda peer: cot_in_ref.at[:, columns(peer, h)],
            got_cot.at[h, my_rows],
        )
        own = keep(5 + h, frozen_ref.at[:, :, columns(me, h)], got_frozen.at[h, me])
        cots.append(
            keep(5 + slabs + h, cot_in_ref.at[:, columns(me, h)], got_cot.at[h, my_rows])
        )
        return [own] + frozens, cots

    places = everyone(1, lambda peer: pos_ref, place_all.at[me])
    coming = fetch(0)
    place_all[me] = pos_ref[...]
    low_parts[tp_me] = fdot(down_ref[...], tokens_ref[...], ((1,), (1,)))
    swaps = tp_swap(0, low_parts)

    start_col[...] = doc_starts(
        lax.broadcasted_iota(jnp.int32, start_col.shape, 0), lengths_ref
    )
    start_row[...] = doc_starts(
        lax.broadcasted_iota(jnp.int32, start_row.shape, 1), lengths_ref
    )
    finish(swaps)
    low_own[...] = tidy(low_parts, low_parts.shape[0]).astype(bf16)
    low_all[me] = low_own[...]
    lows = everyone(2, lambda peer: low_own, low_all.at[me])

    tap_id = lax.broadcasted_iota(jnp.int32, (taps, wide), 0)
    spot_id = lax.broadcasted_iota(jnp.int32, (taps, wide), 1)
    own_filter = filter_ref[part_of(me, groups), :]
    taps_f[...] = fdot(own_filter, jnp.where(tap_id + spot_id == taps, 1.0, 0.0).astype(bf16))
    taps_b[...] = fdot(own_filter, jnp.where(tap_id == spot_id, 1.0, 0.0).astype(bf16))
    for g in range(groups):
        span = slice(g * taps, (g + 1) * taps)
        for taps_ref, bank in ((taps_f, bank_f), (taps_b, bank_b)):
            line = jnp.broadcast_to(taps_ref[g : g + 1, :], (taps, wide))
            bank[span, :] = pltpu.roll(line, 0, 1, stride=1, stride_axis=0).astype(bf16)
    finish(places)

    @pl.loop(0, shards)
    def _(w):
        base = pl.multiple_of(w * rows, rows)
        spot = lax.broadcasted_iota(jnp.int32, (rows, rows), 0) + base
        for j in range(shards):
            hot_ref[pl.ds(base, rows), j * rows : (j + 1) * rows] = jnp.where(
                place_all[j] == spot, 1.0, 0.0
            ).astype(bf16)

    pre[:EDGE, :] = jnp.zeros((EDGE, width), bf16)
    prod[:taps, :] = jnp.zeros((taps, lanes), bf16)
    back[n:, :] = jnp.zeros((taps, lanes), bf16)
    back_post[n:, :] = jnp.zeros((EDGE, width), bf16)
    small_own[...] = jnp.zeros_like(small_own)
    unit = jnp.where(
        lax.broadcasted_iota(jnp.int32, (rank, LANES), 0)
        == lax.broadcasted_iota(jnp.int32, (rank, LANES), 1),
        1.0,
        0.0,
    ).astype(bf16)
    lane_group = lax.broadcasted_iota(jnp.int32, (taps, lanes), 1) // per
    sel = [jnp.where(lane_group == g, 1.0, 0.0).astype(bf16) for g in range(some)]
    turned = wide - 1 - lax.broadcasted_iota(jnp.int32, (taps, wide), 1)
    flip = jnp.where(
        lax.broadcasted_iota(jnp.int32, (wide, wide), 0)
        + lax.broadcasted_iota(jnp.int32, (wide, wide), 1)
        == wide - 1,
        1.0,
        0.0,
    ).astype(bf16)

    def pick(stacked):
        chosen = stacked[:taps]
        for g in range(1, some):
            chosen = jnp.where(lane_group == g, stacked[g * taps : (g + 1) * taps], chosen)
        return chosen

    finish(lows)
    outs = []
    for h in range(slabs):
        frozens, cots = coming
        here = columns(me, h)
        slab = slice(h * lanes, (h + 1) * lanes)
        bank_rows = slice(h * some * taps, (h + 1) * some * taps)
        short_rows = [
            jnp.concatenate([short_ref[s * kinds + a : s * kinds + a + 1, here] for a in range(kinds)], axis=1)
            for s in range(shorts)
        ]
        up_parts = [up_ref[a, :, here] for a in range(kinds)]
        skip = skip_ref[:, here]

        for d in range(shards):
            frozens[d].wait()
            j = lax.rem(me + shards - d, shards)
            at = part_of(j, rows)
            low = low_all[j]
            for a in range(kinds):
                cols = slice(a * lanes, (a + 1) * lanes)
                rhs[at, cols] = (
                    got_frozen[h, j, a].astype(f32) + fdot(low, up_parts[a], ((0,), (0,)))
                ).astype(bf16)
            if h == 0:
                rhs[at, width:] = fdot(low, unit, ((0,), (0,))).astype(bf16)
        if h + 1 < slabs:
            coming = fetch(h + 1)
        tall = rows * 2

        @pl.loop(0, n // tall)
        def _(w):
            base = pl.multiple_of(w * tall, tall)
            at = pl.ds(base, tall)
            to = pl.ds(pl.multiple_of(base + EDGE, EDGE), tall)
            if h == 0:
                moved = fdot(hot_ref[at, :], rhs[...]).astype(bf16)
                pre[to, :] = moved[:, :width]
                low_win[at, :] = moved[:, width:]
            else:
                pre[to, :] = fdot(hot_ref[at, :], rhs[:, :width]).astype(bf16)

        finish(cots)

        @pl.loop(0, blocks)
        def _(b):
            base = pl.multiple_of(b * taps, taps)
            at = pl.ds(base, taps)
            ext = pre[pl.ds(base, taps + EDGE), :].astype(f32)
            off = lax.broadcasted_iota(jnp.int32, (taps, 1), 0) + base - start_col[at, :]
            total = jnp.zeros((taps, width), f32)
            for s in range(shorts):
                gate = (off >= s).astype(f32)
                total = total + short_rows[s] * ext[EDGE - s : EDGE - s + taps] * gate
            rounded = total.astype(bf16)
            post[at, :] = rounded
            rounded = rounded.astype(f32)
            prod[pl.ds(pl.multiple_of(base + taps, taps), taps), :] = (
                rounded[:, lanes : 2 * lanes] * rounded[:, 2 * lanes :]
            ).astype(bf16)
            back[at, :] = (got_cot[h, at, :].astype(f32) * rounded[:, :lanes]).astype(bf16)

        pair_acc[...] = jnp.zeros_like(pair_acc)

        @pl.loop(0, blocks)
        def _(b):
            base = pl.multiple_of(b * taps, taps)
            at = pl.ds(base, taps)
            window = prod[pl.ds(base, 2 * taps), :]
            ahead = back[pl.ds(base, 2 * taps), :]
            begin = start_col[at, :]
            col_pos = lax.broadcasted_iota(jnp.int32, (taps, wide), 1) + (base - taps)
            gate_f = jnp.where(col_pos >= begin, 1.0, 0.0).astype(bf16)
            gate_r = jnp.where(turned + (base - taps) >= begin, 1.0, 0.0)
            row_pos = lax.broadcasted_iota(jnp.int32, (taps, wide), 0) + base
            gate_b = jnp.where(row_pos >= start_row[:, pl.ds(base, wide)], 1.0, 0.0).astype(bf16)
            many_f = jnp.concatenate([gate_f] * some, axis=0)
            many_b = jnp.concatenate([gate_b] * some, axis=0)
            conv = pick(fdot(bank_f[bank_rows, :] * many_f, window))
            spread = pick(fdot(bank_b[bank_rows, :] * many_b, ahead))
            back_here = ahead[:taps]
            split = jnp.concatenate([back_here * sel[g] for g in range(some)], axis=0)
            pairs = fdot(split, fdot(flip, window).astype(bf16), ((1,), (1,)))
            for g in range(some):
                span = slice(g * taps, (g + 1) * taps)
                pair_acc[span, :] += pairs[span] * gate_r
            product = window[taps:].astype(f32)
            cot = got_cot[h, at, :].astype(f32)
            query = post[at, :lanes].astype(f32)
            key = post[at, lanes : 2 * lanes].astype(f32)
            value = post[at, 2 * lanes :].astype(f32)
            gated = cot * query
            direct = conv + skip * product
            out_buf[h, at, :] = (query * direct).astype(bf16)
            product_back = spread + skip * gated
            skip_row = shorts * kinds
            small_own[skip_row : skip_row + 1, slab] += jnp.sum(gated * product, axis=0, keepdims=True)
            back_post[at, :lanes] = (cot * direct).astype(bf16)
            back_post[at, lanes : 2 * lanes] = (product_back * value).astype(bf16)
            back_post[at, 2 * lanes :] = (product_back * key).astype(bf16)

        outs += everyone(
            9 + h, lambda peer: out_buf.at[h, part_of(peer, rows)], mixer_out.at[:, here]
        )
        outs.append(keep(5 + 2 * slabs + h, out_buf.at[h, my_rows], mixer_out.at[:, here]))

        for g in range(some):
            span = slice(g * taps, (g + 1) * taps)
            square = pltpu.roll(pair_acc[span, :], wide - taps + 1, 1, stride=1, stride_axis=0)
            row = h * some + g
            long_own[row : row + 1, :] = jnp.sum(square[:, :taps], axis=0, keepdims=True)

        @pl.loop(0, blocks)
        def _(b):
            base = pl.multiple_of(b * taps, taps)
            at = pl.ds(base, taps)
            ext = pre[pl.ds(base, taps + EDGE), :].astype(f32)
            back_ext = back_post[pl.ds(base, taps + EDGE), :].astype(f32)
            off = (
                lax.broadcasted_iota(jnp.int32, (taps + EDGE, 1), 0)
                + base
                - start_col[pl.ds(base, taps + EDGE), :]
            )
            total = jnp.zeros((taps, width), f32)
            for s in range(shorts):
                masked = back_ext * (off >= s).astype(f32)
                total = total + short_rows[s] * masked[s : s + taps]
                sums = jnp.sum(
                    masked[:taps] * ext[EDGE - s : EDGE - s + taps], axis=0, keepdims=True
                )
                for a in range(kinds):
                    row = s * kinds + a
                    small_own[row : row + 1, slab] += sums[:, a * lanes : (a + 1) * lanes]
            rhs[at, :width] = total.astype(bf16)

        back_pre = rhs[:, :width]
        low_term = fdot(jnp.concatenate(up_parts, axis=1), back_pre, ((1,), (1,)))
        back_low[...] = low_term if h == 0 else back_low[...] + low_term
        if h + 1 == slabs:
            reduce_low = everyone(0, lambda peer: back_low.at[:, part_of(peer, rows)], low_got.at[me])
            low_got[me] = back_low[:, my_rows]
        up_term = fdot(low_win[...], back_pre, ((0,), (0,)))
        for a in range(kinds):
            up_own[a, :, slab] = up_term[:rank, a * lanes : (a + 1) * lanes]

    copies = everyone(3, lambda peer: up_own, grad_up.at[:, :, mine])
    copies += everyone(4, lambda peer: small_own, grad_small.at[:, mine])
    copies += everyone(5, lambda peer: long_own, grad_long.at[part_of(me, groups)])
    copies += outs
    copies.append(keep(1, up_own, grad_up.at[:, :, mine]))
    copies.append(keep(2, small_own, grad_small.at[:, mine]))
    copies.append(keep(3, long_own, grad_long.at[part_of(me, groups)]))
    finish(reduce_low)
    back_parts[tp_me] = tidy(low_got, shards)
    finish(tp_swap(1, back_parts))
    back_own_low[...] = tidy(back_parts, back_parts.shape[0]).astype(bf16)
    back_all[me] = back_own_low[...]
    finish(everyone(6, lambda peer: back_own_low, back_all.at[me]))
    back_own = jnp.zeros((rank, rows), f32)
    for j in range(shards):
        spot = lax.broadcasted_iota(jnp.int32, (rows, rows), 0) + j * rows
        hot = jnp.where(pos_ref[...] == spot, 1.0, 0.0).astype(bf16)
        back_own = back_own + fdot(back_all[j], hot)
    down_part[...] = fdot(back_own.astype(bf16), tokens_ref[...])
    reduce_down = everyone(7, lambda peer: down_part.at[:, part_of(peer, c)], down_got.at[me])
    down_got[me] = down_part[:, mine]
    finish(reduce_down)
    down_own[...] = tidy(down_got, shards)
    copies += everyone(8, lambda peer: down_own, grad_down.at[:, mine])
    copies.append(keep(4, down_own, grad_down.at[:, mine]))
    finish(copies)


def mixer(lengths, frozen, cot, tokens, down, pos, up, short, long_filter, skip):
    kinds, rows, channels = frozen.shape
    shards, tps = lax.axis_size("ctx"), lax.axis_size("tp")
    n, c = rows * shards, channels // shards
    slabs, lanes = c // LANES, LANES
    taps = long_filter.shape[1]
    groups, wide = long_filter.shape[0] // shards, 2 * taps
    width = kinds * lanes
    rank = down.shape[0]
    small = -(-(short.shape[0] + 1) // 8) * 8
    f32, bf16, i32 = jnp.float32, jnp.bfloat16, jnp.int32
    shape = jax.ShapeDtypeStruct
    vmem, hbm = pl.BlockSpec(memory_space=pltpu.VMEM), pl.BlockSpec(memory_space=pl.ANY)
    return pl.pallas_call(
        mixer_kernel,
        out_shape=(
            shape((rows, channels), bf16),
            shape((rank, channels), f32),
            shape((kinds, rank, channels), f32),
            shape((small, channels), f32),
            shape((shards * groups, taps), f32),
        ),
        in_specs=[pl.BlockSpec(memory_space=pltpu.SMEM), hbm, hbm] + [vmem] * 7,
        out_specs=(hbm,) * 5,
        scratch_shapes=[
            pltpu.VMEM((slabs, shards, kinds, rows, lanes), bf16),
            pltpu.VMEM((slabs, n, lanes), bf16),
            pltpu.VMEM((shards, rank, rows), bf16),
            pltpu.VMEM((shards, 1, rows), i32),
            pltpu.VMEM((slabs, n, lanes), bf16),
            pltpu.VMEM((kinds, rank, c), f32),
            pltpu.VMEM((small, c), f32),
            pltpu.VMEM((groups, taps), f32),
            pltpu.VMEM((rank, n), f32),
            pltpu.VMEM((shards, rank, rows), f32),
            pltpu.VMEM((tps, rank, rows), f32),
            pltpu.VMEM((rank, rows), bf16),
            pltpu.VMEM((shards, rank, rows), bf16),
            pltpu.VMEM((rank, channels), f32),
            pltpu.VMEM((shards, rank, c), f32),
            pltpu.VMEM((rank, c), f32),
            pltpu.VMEM((tps, rank, rows), f32),
            pltpu.VMEM((rank, rows), bf16),
            pltpu.VMEM((n, n), bf16),
            pltpu.VMEM((n, width + LANES), bf16),
            pltpu.VMEM((n + EDGE, width), bf16),
            pltpu.VMEM((n, LANES), bf16),
            pltpu.VMEM((n, width), bf16),
            pltpu.VMEM((n + taps, lanes), bf16),
            pltpu.VMEM((n + taps, lanes), bf16),
            pltpu.VMEM((n + EDGE, width), bf16),
            pltpu.VMEM((groups, wide), f32),
            pltpu.VMEM((groups, wide), f32),
            pltpu.VMEM((groups * taps, wide), bf16),
            pltpu.VMEM((groups * taps, wide), bf16),
            pltpu.VMEM((groups // slabs * taps, wide), f32),
            pltpu.VMEM((n + EDGE, 1), i32),
            pltpu.VMEM((1, n + taps), i32),
            pltpu.SemaphoreType.DMA((9 + 3 * slabs, shards)),
            pltpu.SemaphoreType.DMA((9 + 3 * slabs, shards)),
            pltpu.SemaphoreType.DMA((5 + 3 * slabs,)),
            pltpu.SemaphoreType.DMA((2, tps)),
            pltpu.SemaphoreType.DMA((2, tps)),
        ],
        compiler_params=pltpu.CompilerParams(
            collective_id=0, has_side_effects=True, vmem_limit_bytes=58 * 1024 * 1024
        ),
        cost_estimate=pl.CostEstimate(
            flops=8 * n * groups * taps * wide, bytes_accessed=16 * n * c, transcendentals=0
        ),
    )(lengths, frozen, cot, tokens, down, pos, up, short, long_filter, skip)


def by_channels(
    tokens,
    frozen,
    cotangent,
    adapter_down_weight,
    adapter_up_weight,
    short_depthwise_filter,
    long_group_filter,
    skip_direct_scale,
    document_lengths,
    window_row_position,
):
    channels = tokens.shape[1]
    shorts, kinds, _ = short_depthwise_filter.shape
    count = shorts * kinds
    mixer_out, grad_down, grad_up, grad_small, grad_long = mixer(
        document_lengths,
        frozen.transpose(1, 0, 2),
        cotangent,
        tokens,
        adapter_down_weight,
        window_row_position[None, :],
        adapter_up_weight.transpose(1, 0, 2),
        short_depthwise_filter.reshape(count, channels).astype(jnp.float32),
        long_group_filter,
        skip_direct_scale[None, :],
    )
    return (
        mixer_out,
        grad_down,
        grad_up.transpose(1, 0, 2),
        grad_small[:count].reshape(shorts, kinds, channels),
        grad_long,
        grad_small[count],
    )


def from_behind(value, axis, steps):
    count = lax.axis_size(axis)
    first, last = (max(0, -steps), min(count, count - steps))
    return lax.ppermute(value, axis, [(source, source + steps) for source in range(first, last)])


def doc_offsets(positions, document_lengths):
    doc_ends = jnp.cumsum(document_lengths)
    starts = doc_ends - document_lengths
    clipped = jnp.maximum(positions, 0)
    begins = jnp.max(jnp.where(starts[None, :] <= clipped[:, None], starts[None, :], 0), axis=1)
    return clipped - begins


def tap_mask(offsets, shift_tap, ndim):
    return (shift_tap <= offsets).astype(jnp.float32).reshape((-1,) + (1,) * (ndim - 1))


def pick_rows(source, row_index):
    padded = jnp.concatenate([source, jnp.zeros((1,) + source.shape[1:], source.dtype)])
    return jnp.take(padded, row_index, axis=0)


def short_apply(extended, filter_taps, offsets):
    length = offsets.shape[0]
    taps = filter_taps.shape[0]
    reach = taps - 1
    running = jnp.zeros((length,) + extended.shape[1:], jnp.float32)
    for shift_tap in range(taps):
        shifted = extended[reach - shift_tap : reach - shift_tap + length].astype(jnp.float32)
        running = running + filter_taps[shift_tap].astype(jnp.float32) * shifted * tap_mask(
            offsets, shift_tap, extended.ndim
        )
    return running


def short_back(back_ext, filter_taps, offsets_ext):
    taps = filter_taps.shape[0]
    length = back_ext.shape[0] - (taps - 1)
    running = jnp.zeros((length,) + back_ext.shape[1:], jnp.float32)
    for shift_tap in range(taps):
        shifted = back_ext[shift_tap : shift_tap + length].astype(jnp.float32)
        masked = shifted * tap_mask(
            offsets_ext[shift_tap : shift_tap + length], shift_tap, back_ext.ndim
        )
        running = running + filter_taps[shift_tap].astype(jnp.float32) * masked
    return running


def short_grad(back_post, pre_ext, offsets, taps):
    length = offsets.shape[0]
    reach = taps - 1
    back_float = back_post.astype(jnp.float32)
    collected = []
    for shift_tap in range(taps):
        shifted = pre_ext[reach - shift_tap : reach - shift_tap + length].astype(jnp.float32)
        collected.append(
            jnp.sum(back_float * shifted * tap_mask(offsets, shift_tap, pre_ext.ndim), axis=0)
        )
    return jnp.stack(collected)


def toeplitz(filter_bank):
    groups = filter_bank.shape[0]
    row_vals = jnp.concatenate(
        [
            jnp.zeros((groups, 1), filter_bank.dtype),
            filter_bank[:, ::-1],
            jnp.zeros((groups, 128), filter_bank.dtype),
        ],
        axis=1,
    )
    tiled = jnp.broadcast_to(row_vals[:, None, :], (groups, 128, 257)).reshape(groups, 128 * 257)
    return tiled[:, : 128 * 256].reshape(groups, 128, 256)


def masked_bank(filter_bank, block_off):
    row_ids = jnp.arange(128, dtype=jnp.int32)[:, None]
    col_ids = jnp.arange(256, dtype=jnp.int32)[None, :]
    allowed = (row_ids + 128 - col_ids <= block_off[:, None]).astype(filter_bank.dtype)
    return filter_bank * allowed[None]


def adapter_hidden(row_tile_block, adapter_down_weight):
    partial_low = lax.dot_general(
        adapter_down_weight,
        row_tile_block,
        (((1,), (1,)), ((), ())),
        preferred_element_type=jnp.float32,
    )
    return lax.psum(partial_low, "tp").astype(jnp.bfloat16)


def on_device(
    tokens,
    frozen,
    cotangent,
    adapter_down_weight,
    adapter_up_weight,
    short_depthwise_filter,
    long_group_filter,
    skip_direct_scale,
    document_lengths,
    window_row_position,
):
    local_rows, channels = tokens.shape
    short_count = short_depthwise_filter.shape[0]
    reach = short_count - 1
    groups = channels // 16
    blocks = local_rows // 128
    shards = lax.axis_size("ctx")
    capacity = 2 * local_rows // shards
    my_index = lax.axis_index("ctx")
    first_pos = my_index * local_rows
    all_pos = lax.all_gather(window_row_position, "ctx", axis=0, tiled=True)
    shard_ids = jnp.arange(shards, dtype=jnp.int32)
    own_dest = window_row_position // local_rows
    own_hits = (own_dest[:, None] == shard_ids[None, :]).astype(jnp.int32)
    own_rank = jnp.sum(jnp.cumsum(own_hits, axis=0) * own_hits, axis=1) - 1
    own_slot = own_dest * capacity + own_rank
    send_rows = (
        jnp.full((shards * capacity,), local_rows, jnp.int32)
        .at[own_slot]
        .set(jnp.arange(local_rows, dtype=jnp.int32))
    )
    grid_pos = all_pos.reshape(shards, local_rows)
    arriving = grid_pos // local_rows == my_index
    arrive_rank = jnp.cumsum(arriving.astype(jnp.int32), axis=1) - 1
    arrive_slot = shard_ids[:, None] * capacity + arrive_rank
    local_target = jnp.where(arriving, grid_pos % local_rows, local_rows)
    recv_rows = (
        jnp.zeros((local_rows,), jnp.int32)
        .at[local_target.reshape(-1)]
        .set(arrive_slot.reshape(-1), mode="drop")
    )
    frozen_buf = pick_rows(frozen, send_rows).reshape((shards, capacity) + frozen.shape[1:])
    token_buf = pick_rows(tokens, send_rows).reshape(shards, capacity, channels)
    got_tokens, got_frozen = (
        lax.all_to_all(token_buf, "ctx", split_axis=0, concat_axis=0, tiled=True),
        lax.all_to_all(frozen_buf, "ctx", split_axis=0, concat_axis=0, tiled=True),
    )
    packed_token_rows = jnp.take(got_tokens.reshape(shards * capacity, channels), recv_rows, axis=0)
    packed_frozen = jnp.take(
        got_frozen.reshape((shards * capacity,) + frozen.shape[1:]), recv_rows, axis=0
    )
    lowrank_product = adapter_hidden(packed_token_rows, adapter_down_weight)
    before_convolution = (
        packed_frozen.astype(jnp.float32)
        + jnp.einsum(
            "ed,ejg->djg", lowrank_product, adapter_up_weight, preferred_element_type=jnp.float32
        )
    ).astype(jnp.bfloat16)
    positions = first_pos - 127 + jnp.arange(local_rows + 255, dtype=jnp.int32)
    offsets_all = doc_offsets(positions, document_lengths)
    own_off = offsets_all[127 : 127 + local_rows]
    pre_edge = from_behind(before_convolution[-reach:], "ctx", 1)
    pre_ext = jnp.concatenate([pre_edge, before_convolution])
    post_conv = short_apply(pre_ext, short_depthwise_filter, own_off).astype(jnp.bfloat16)
    product = (post_conv[:, 1].astype(jnp.float32) * post_conv[:, 2].astype(jnp.float32)).astype(
        jnp.bfloat16
    )
    product_edge = from_behind(product[-127:], "ctx", 1)
    product_ext = jnp.concatenate([jnp.zeros((1, channels), jnp.bfloat16), product_edge, product])
    filter_bank = toeplitz(long_group_filter)
    windows = jnp.concatenate(
        [
            product_ext[:-128].reshape(blocks, 128, channels),
            product_ext[128:].reshape(blocks, 128, channels),
        ],
        axis=1,
    )
    block_offsets = own_off.reshape(blocks, 128)

    def forward_block(pieces):
        window_rows, block_off = pieces
        masked = masked_bank(filter_bank, block_off)
        return jnp.einsum(
            "gij,jgc->igc",
            masked,
            window_rows.reshape(256, groups, 16),
            preferred_element_type=jnp.float32,
        ).reshape(128, channels)

    convolved = lax.map(forward_block, (windows, block_offsets)).reshape(local_rows, channels)
    query_rows = post_conv[:, 0].astype(jnp.float32)
    key_rows = post_conv[:, 1].astype(jnp.float32)
    value_rows = post_conv[:, 2].astype(jnp.float32)
    product_float = product.astype(jnp.float32)
    direct_term = convolved + skip_direct_scale[None, :] * product_float
    mixer_out = (query_rows * direct_term).astype(jnp.bfloat16)
    grad_float = cotangent.astype(jnp.float32)
    gated_back = grad_float * query_rows
    back_conv = gated_back.astype(jnp.bfloat16)
    conv_edge = from_behind(back_conv[:127], "ctx", -1)
    edge_block = jnp.concatenate([conv_edge, jnp.zeros((1, channels), jnp.bfloat16)])

    def backward_block(pieces):
        window_rows, conv_rows, block_off = pieces
        masked = masked_bank(filter_bank, block_off)
        split_conv = conv_rows.reshape(128, groups, 16)
        spread = jnp.einsum(
            "gij,igc->jgc", masked, split_conv, preferred_element_type=jnp.float32
        ).reshape(256, channels)
        pair_sums = jnp.einsum(
            "igc,jgc->gij",
            split_conv,
            window_rows.reshape(256, groups, 16),
            preferred_element_type=jnp.float32,
        )
        skewed = jnp.pad(pair_sums.reshape(groups, 128 * 256), ((0, 0), (0, 128))).reshape(
            groups, 128, 257
        )[:, :, 1:129][:, :, ::-1]
        allowed = (jnp.arange(128, dtype=jnp.int32)[None, :] <= block_off[:, None]).astype(
            jnp.float32
        )
        return (spread, jnp.sum(skewed * allowed[None], axis=1))

    spread_all, filter_parts = lax.map(
        backward_block, (windows, back_conv.reshape(blocks, 128, channels), block_offsets)
    )
    edge_off = offsets_all[127 + local_rows : 127 + local_rows + 128]
    edge_bank = masked_bank(filter_bank, edge_off)[:, :, :128]
    edge_spread = jnp.einsum(
        "gij,igc->jgc",
        edge_bank,
        edge_block.reshape(128, groups, 16),
        preferred_element_type=jnp.float32,
    ).reshape(128, channels)
    following = jnp.concatenate([spread_all[1:, :128], edge_spread[None]], axis=0).reshape(
        local_rows, channels
    )
    product_back = (
        spread_all[:, 128:].reshape(local_rows, channels)
        + following
        + skip_direct_scale[None, :] * gated_back
    )
    grad_long = jnp.sum(filter_parts, axis=0)
    grad_skip = jnp.sum(gated_back * product_float, axis=0)
    query_back = grad_float * direct_term
    back_post = jnp.stack(
        [query_back, product_back * value_rows, product_back * key_rows], axis=1
    ).astype(jnp.bfloat16)
    post_edge = from_behind(back_post[:reach], "ctx", -1)
    back_ext = jnp.concatenate([back_post, post_edge])
    gradient_before_filter = short_back(
        back_ext, short_depthwise_filter, offsets_all[127 : 127 + local_rows + reach]
    ).astype(jnp.bfloat16)
    grad_short = short_grad(back_post, pre_ext, own_off, short_count)
    up_gradient = jnp.einsum(
        "kp,pme->kme", lowrank_product, gradient_before_filter, preferred_element_type=jnp.float32
    )
    partial_gradient = jnp.einsum(
        "ldx,idx->li", adapter_up_weight, gradient_before_filter, preferred_element_type=jnp.float32
    )
    back_low = lax.psum(partial_gradient, "tp").astype(jnp.bfloat16)
    grad_down = jnp.dot(back_low, packed_token_rows, preferred_element_type=jnp.float32)
    summed = lax.psum((grad_down, up_gradient, grad_short, grad_long, grad_skip), "ctx")
    return (mixer_out,) + tuple(summed)


def solution(mesh):
    placed = (
        P("ctx", "tp"),
        P("ctx", None, "tp"),
        P("ctx", "tp"),
        P(None, "tp"),
        P(None, None, "tp"),
        P(None, None, "tp"),
        P("tp", None),
        P("tp"),
        P(),
        P("ctx"),
    )
    channels_each = mesh.shape["ctx"] * LANES

    def run(*args):
        fits = args[0].shape[1] % channels_each == 0
        return (by_channels if fits else on_device)(*args)

    return jax.shard_map(
        run,
        mesh=mesh,
        in_specs=placed,
        out_specs=(
            P("ctx", "tp"),
            P(None, "tp"),
            P(None, None, "tp"),
            P(None, None, "tp"),
            P("tp", None),
            P("tp"),
        ),
        check_vma=False,
    )
```

```python
import functools

import jax
import jax.numpy as jnp
from jax import lax
from jax.experimental import pallas as pl
from jax.experimental.pallas import tpu as pltpu
from jax.sharding import PartitionSpec as P

EDGE = 16
LANES = 128


def fdot(left, right, contract=((1,), (0,))):
    return lax.dot_general(left, right, (contract, ((), ())), preferred_element_type=jnp.float32)


def doc_starts(pos, lengths_ref):
    begins = jnp.zeros_like(pos)
    running = jnp.int32(0)
    for doc in range(lengths_ref.shape[0]):
        begins = jnp.where(pos >= running, running, begins)
        running = running + lengths_ref[doc]
    return begins


def ctx_peers():
    me, count = lax.axis_index("ctx"), lax.axis_size("ctx")
    return me, [(d, lax.rem(me + d, count)) for d in range(1, count)]


def tp_peers():
    me, count = lax.axis_index("tp"), lax.axis_size("tp")
    return me, [(d, lax.rem(me + d, count)) for d in range(1, count)]


def greet():
    barrier = pltpu.get_barrier_semaphore()
    waits = 0
    for axis, (_, peers) in (("ctx", ctx_peers()), ("tp", tp_peers())):
        for _, peer in peers:
            pl.semaphore_signal(
                barrier, inc=1, device_id={axis: peer}, device_id_type=pl.DeviceIdType.MESH
            )
            waits += 1
    pl.semaphore_wait(barrier, waits)


def push(src, dst, send_sem, recv_sem, axis, peer):
    copy = pltpu.make_async_remote_copy(
        src_ref=src,
        dst_ref=dst,
        send_sem=send_sem,
        recv_sem=recv_sem,
        device_id={axis: peer},
        device_id_type=pl.DeviceIdType.MESH,
    )
    copy.start()
    return copy


def part_of(index, size):
    return pl.ds(pl.multiple_of(index * size, size), size)


def mixer_kernel(
    lengths_ref,
    frozen_ref,
    cot_in_ref,
    tokens_ref,
    down_ref,
    pos_ref,
    up_ref,
    short_ref,
    filter_ref,
    skip_ref,
    mixer_out,
    grad_down,
    grad_up,
    grad_small,
    grad_long,
    got_frozen,
    got_cot,
    low_all,
    place_all,
    out_buf,
    up_own,
    small_own,
    long_own,
    back_low,
    low_got,
    back_parts,
    back_own_low,
    back_all,
    down_part,
    down_got,
    down_own,
    low_parts,
    low_own,
    hot_ref,
    rhs,
    pre,
    low_win,
    post,
    prod,
    back,
    back_post,
    taps_f,
    taps_b,
    bank_f,
    bank_b,
    pair_acc,
    start_col,
    start_row,
    send_sems,
    recv_sems,
    own_sems,
    tp_send,
    tp_recv,
):
    slabs, shards, kinds, rows, lanes = got_frozen.shape
    n, c = rows * shards, lanes * slabs
    groups, wide = taps_f.shape
    taps = wide // 2
    per = c // groups
    some = groups // slabs
    width = kinds * lanes
    blocks = n // taps
    shorts = short_ref.shape[0]
    rank = down_ref.shape[0]
    f32, bf16 = jnp.float32, jnp.bfloat16
    me, peers = ctx_peers()
    tp_me, tp_others = tp_peers()
    mine, my_rows = part_of(me, c), part_of(me, rows)
    greet()

    def everyone(step, source, target):
        return [
            push(source(peer), target, send_sems.at[step, d], recv_sems.at[step, d], "ctx", peer)
            for d, peer in peers
        ]

    def tp_swap(step, parts):
        return [
            push(
                parts.at[tp_me],
                parts.at[tp_me],
                tp_send.at[step, d],
                tp_recv.at[step, d],
                "tp",
                peer,
            )
            for d, peer in tp_others
        ]

    def keep(step, source, target):
        copy = pltpu.make_async_copy(source, target, own_sems.at[step])
        copy.start()
        return copy

    def finish(copies):
        for copy in copies:
            copy.wait()

    def tidy(parts, count):
        total = parts[0]
        for t in range(1, count):
            total = total + parts[t]
        return total

    def columns(index, h):
        return pl.ds(pl.multiple_of(index * c + h * lanes, lanes), lanes)

    def fetch_frozen(h):
        own = keep(5 + h, frozen_ref.at[:, :, columns(me, h)], got_frozen.at[h, me])
        return [own] + everyone(
            9 + slabs + h, lambda peer: frozen_ref.at[:, :, columns(peer, h)], got_frozen.at[h, me]
        )

    def fetch_cot(h):
        own = keep(5 + slabs + h, cot_in_ref.at[:, columns(me, h)], got_cot.at[h, my_rows])
        return [own] + everyone(
            9 + 2 * slabs + h,
            lambda peer: cot_in_ref.at[:, columns(peer, h)],
            got_cot.at[h, my_rows],
        )

    places = everyone(1, lambda peer: pos_ref, place_all.at[me])
    coming = fetch_frozen(0)
    place_all[me] = pos_ref[...]
    low_parts[tp_me] = fdot(down_ref[...], tokens_ref[...], ((1,), (1,)))
    swaps = tp_swap(0, low_parts)

    start_col[...] = doc_starts(
        lax.broadcasted_iota(jnp.int32, start_col.shape, 0), lengths_ref
    )
    start_row[...] = doc_starts(
        lax.broadcasted_iota(jnp.int32, start_row.shape, 1), lengths_ref
    )
    finish(swaps)
    low_own[...] = tidy(low_parts, low_parts.shape[0]).astype(bf16)
    low_all[me] = low_own[...]
    lows = everyone(2, lambda peer: low_own, low_all.at[me])

    tap_id = lax.broadcasted_iota(jnp.int32, (taps, wide), 0)
    spot_id = lax.broadcasted_iota(jnp.int32, (taps, wide), 1)
    own_filter = filter_ref[part_of(me, groups), :]
    taps_f[...] = fdot(own_filter, jnp.where(tap_id + spot_id == taps, 1.0, 0.0).astype(bf16))
    taps_b[...] = fdot(own_filter, jnp.where(tap_id == spot_id, 1.0, 0.0).astype(bf16))
    for g in range(groups):
        span = slice(g * taps, (g + 1) * taps)
        for taps_ref, bank in ((taps_f, bank_f), (taps_b, bank_b)):
            line = jnp.broadcast_to(taps_ref[g : g + 1, :], (taps, wide))
            bank[span, :] = pltpu.roll(line, 0, 1, stride=1, stride_axis=0).astype(bf16)
    finish(places)

    @pl.loop(0, shards)
    def _(w):
        base = pl.multiple_of(w * rows, rows)
        spot = lax.broadcasted_iota(jnp.int32, (rows, rows), 0) + base
        for j in range(shards):
            hot_ref[pl.ds(base, rows), j * rows : (j + 1) * rows] = jnp.where(
                place_all[j] == spot, 1.0, 0.0
            ).astype(bf16)

    pre[:EDGE, :] = jnp.zeros((EDGE, width), bf16)
    prod[:taps, :] = jnp.zeros((taps, lanes), bf16)
    back[n:, :] = jnp.zeros((taps, lanes), bf16)
    back_post[n:, :] = jnp.zeros((EDGE, width), bf16)
    small_own[...] = jnp.zeros_like(small_own)
    unit = jnp.where(
        lax.broadcasted_iota(jnp.int32, (rank, LANES), 0)
        == lax.broadcasted_iota(jnp.int32, (rank, LANES), 1),
        1.0,
        0.0,
    ).astype(bf16)
    lane_group = lax.broadcasted_iota(jnp.int32, (taps, lanes), 1) // per
    sel = [jnp.where(lane_group == g, 1.0, 0.0).astype(bf16) for g in range(some)]
    turned = wide - 1 - lax.broadcasted_iota(jnp.int32, (taps, wide), 1)
    flip = jnp.where(
        lax.broadcasted_iota(jnp.int32, (wide, wide), 0)
        + lax.broadcasted_iota(jnp.int32, (wide, wide), 1)
        == wide - 1,
        1.0,
        0.0,
    ).astype(bf16)

    def pick(stacked):
        chosen = stacked[:taps]
        for g in range(1, some):
            chosen = jnp.where(lane_group == g, stacked[g * taps : (g + 1) * taps], chosen)
        return chosen

    finish(lows)
    outs = []
    for h in range(slabs):
        frozens = coming
        here = columns(me, h)
        slab = slice(h * lanes, (h + 1) * lanes)
        bank_rows = slice(h * some * taps, (h + 1) * some * taps)
        short_rows = []
        for s in range(shorts):
            lines = short_ref[s, :, here].astype(f32)
            short_rows.append(
                jnp.concatenate([lines[a : a + 1] for a in range(kinds)], axis=1)
            )
        up_parts = [up_ref[a, :, here] for a in range(kinds)]
        skip = skip_ref[:, here]

        for d in range(shards):
            frozens[d].wait()
            j = lax.rem(me + shards - d, shards)
            at = part_of(j, rows)
            low = low_all[j]
            for a in range(kinds):
                cols = slice(a * lanes, (a + 1) * lanes)
                rhs[at, cols] = (
                    got_frozen[h, j, a].astype(f32) + fdot(low, up_parts[a], ((0,), (0,)))
                ).astype(bf16)
            if h == 0:
                rhs[at, width:] = fdot(low, unit, ((0,), (0,))).astype(bf16)
        if h == 0:
            cots = fetch_cot(0)
        tall = rows * 2

        @pl.loop(0, n // tall)
        def _(w):
            base = pl.multiple_of(w * tall, tall)
            at = pl.ds(base, tall)
            to = pl.ds(pl.multiple_of(base + EDGE, EDGE), tall)
            if h == 0:
                moved = fdot(hot_ref[at, :], rhs[...]).astype(bf16)
                pre[to, :] = moved[:, :width]
                low_win[at, :] = moved[:, width:]
            else:
                pre[to, :] = fdot(hot_ref[at, :], rhs[:, :width]).astype(bf16)

        finish(cots)
        if h + 1 < slabs:
            coming = fetch_frozen(h + 1)
            cots = fetch_cot(h + 1)

        @pl.loop(0, blocks)
        def _(b):
            base = pl.multiple_of(b * taps, taps)
            at = pl.ds(base, taps)
            ext = pre[pl.ds(base, taps + EDGE), :].astype(f32)
            off = lax.broadcasted_iota(jnp.int32, (taps, 1), 0) + base - start_col[at, :]
            total = jnp.zeros((taps, width), f32)
            for s in range(shorts):
                gate = (off >= s).astype(f32)
                total = total + short_rows[s] * ext[EDGE - s : EDGE - s + taps] * gate
            rounded = total.astype(bf16)
            post[at, :] = rounded
            rounded = rounded.astype(f32)
            prod[pl.ds(pl.multiple_of(base + taps, taps), taps), :] = (
                rounded[:, lanes : 2 * lanes] * rounded[:, 2 * lanes :]
            ).astype(bf16)
            back[at, :] = (got_cot[h, at, :].astype(f32) * rounded[:, :lanes]).astype(bf16)

        pair_acc[...] = jnp.zeros_like(pair_acc)

        @pl.loop(0, blocks)
        def _(b):
            base = pl.multiple_of(b * taps, taps)
            at = pl.ds(base, taps)
            window = prod[pl.ds(base, 2 * taps), :]
            ahead = back[pl.ds(base, 2 * taps), :]
            begin = start_col[at, :]
            col_pos = lax.broadcasted_iota(jnp.int32, (taps, wide), 1) + (base - taps)
            gate_f = jnp.where(col_pos >= begin, 1.0, 0.0).astype(bf16)
            gate_r = jnp.where(turned + (base - taps) >= begin, 1.0, 0.0)
            row_pos = lax.broadcasted_iota(jnp.int32, (taps, wide), 0) + base
            gate_b = jnp.where(row_pos >= start_row[:, pl.ds(base, wide)], 1.0, 0.0).astype(bf16)
            many_f = jnp.concatenate([gate_f] * some, axis=0)
            many_b = jnp.concatenate([gate_b] * some, axis=0)
            conv = pick(fdot(bank_f[bank_rows, :] * many_f, window))
            spread = pick(fdot(bank_b[bank_rows, :] * many_b, ahead))
            back_here = ahead[:taps]
            split = jnp.concatenate([back_here * sel[g] for g in range(some)], axis=0)
            pairs = fdot(split, fdot(flip, window).astype(bf16), ((1,), (1,)))
            for g in range(some):
                span = slice(g * taps, (g + 1) * taps)
                pair_acc[span, :] += pairs[span] * gate_r
            product = window[taps:].astype(f32)
            cot = got_cot[h, at, :].astype(f32)
            query = post[at, :lanes].astype(f32)
            key = post[at, lanes : 2 * lanes].astype(f32)
            value = post[at, 2 * lanes :].astype(f32)
            gated = cot * query
            direct = conv + skip * product
            out_buf[h, at, :] = (query * direct).astype(bf16)
            product_back = spread + skip * gated
            skip_row = shorts * kinds
            small_own[skip_row : skip_row + 1, slab] += jnp.sum(gated * product, axis=0, keepdims=True)
            back_post[at, :lanes] = (cot * direct).astype(bf16)
            back_post[at, lanes : 2 * lanes] = (product_back * value).astype(bf16)
            back_post[at, 2 * lanes :] = (product_back * key).astype(bf16)

        outs += everyone(
            9 + h, lambda peer: out_buf.at[h, part_of(peer, rows)], mixer_out.at[:, here]
        )
        outs.append(keep(5 + 2 * slabs + h, out_buf.at[h, my_rows], mixer_out.at[:, here]))

        @pl.loop(0, blocks)
        def _(b):
            base = pl.multiple_of(b * taps, taps)
            at = pl.ds(base, taps)
            ext = pre[pl.ds(base, taps + EDGE), :].astype(f32)
            back_ext = back_post[pl.ds(base, taps + EDGE), :].astype(f32)
            off = (
                lax.broadcasted_iota(jnp.int32, (taps + EDGE, 1), 0)
                + base
                - start_col[pl.ds(base, taps + EDGE), :]
            )
            total = jnp.zeros((taps, width), f32)
            for s in range(shorts):
                masked = back_ext * (off >= s).astype(f32)
                total = total + short_rows[s] * masked[s : s + taps]
                sums = jnp.sum(
                    masked[:taps] * ext[EDGE - s : EDGE - s + taps], axis=0, keepdims=True
                )
                for a in range(kinds):
                    row = s * kinds + a
                    small_own[row : row + 1, slab] += sums[:, a * lanes : (a + 1) * lanes]
            rhs[at, :width] = total.astype(bf16)

        back_pre = rhs[:, :width]
        low_term = fdot(jnp.concatenate(up_parts, axis=1), back_pre, ((1,), (1,)))
        back_low[...] = low_term if h == 0 else back_low[...] + low_term
        if h + 1 == slabs:
            reduce_low = everyone(0, lambda peer: back_low.at[:, part_of(peer, rows)], low_got.at[me])
            low_got[me] = back_low[:, my_rows]
        up_term = fdot(low_win[...], back_pre, ((0,), (0,)))
        for a in range(kinds):
            up_own[a, :, slab] = up_term[:rank, a * lanes : (a + 1) * lanes]

        for g in range(some):
            span = slice(g * taps, (g + 1) * taps)
            square = pltpu.roll(pair_acc[span, :], wide - taps + 1, 1, stride=1, stride_axis=0)
            row = h * some + g
            long_own[row : row + 1, :] = jnp.sum(square[:, :taps], axis=0, keepdims=True)

    copies = everyone(3, lambda peer: up_own, grad_up.at[:, :, mine])
    copies += everyone(4, lambda peer: small_own, grad_small.at[:, mine])
    copies += everyone(5, lambda peer: long_own, grad_long.at[part_of(me, groups)])
    copies += outs
    copies.append(keep(1, up_own, grad_up.at[:, :, mine]))
    copies.append(keep(2, small_own, grad_small.at[:, mine]))
    copies.append(keep(3, long_own, grad_long.at[part_of(me, groups)]))
    finish(reduce_low)
    back_parts[tp_me] = tidy(low_got, shards)
    finish(tp_swap(1, back_parts))
    back_own_low[...] = tidy(back_parts, back_parts.shape[0]).astype(bf16)
    back_all[me] = back_own_low[...]
    finish(everyone(6, lambda peer: back_own_low, back_all.at[me]))
    back_own = jnp.zeros((rank, rows), f32)
    for j in range(shards):
        spot = lax.broadcasted_iota(jnp.int32, (rows, rows), 0) + j * rows
        hot = jnp.where(pos_ref[...] == spot, 1.0, 0.0).astype(bf16)
        back_own = back_own + fdot(back_all[j], hot)
    down_part[...] = fdot(back_own.astype(bf16), tokens_ref[...])
    reduce_down = everyone(7, lambda peer: down_part.at[:, part_of(peer, c)], down_got.at[me])
    down_got[me] = down_part[:, mine]
    finish(reduce_down)
    down_own[...] = tidy(down_got, shards)
    copies += everyone(8, lambda peer: down_own, grad_down.at[:, mine])
    copies.append(keep(4, down_own, grad_down.at[:, mine]))
    finish(copies)


def mixer(lengths, frozen, cot, tokens, down, pos, up, short, long_filter, skip):
    kinds, rows, channels = frozen.shape
    shards, tps = lax.axis_size("ctx"), lax.axis_size("tp")
    n, c = rows * shards, channels // shards
    slabs, lanes = c // LANES, LANES
    taps = long_filter.shape[1]
    groups, wide = long_filter.shape[0] // shards, 2 * taps
    width = kinds * lanes
    rank = down.shape[0]
    small = -(-(short.shape[0] * kinds + 1) // 8) * 8
    f32, bf16, i32 = jnp.float32, jnp.bfloat16, jnp.int32
    shape = jax.ShapeDtypeStruct
    vmem, hbm = pl.BlockSpec(memory_space=pltpu.VMEM), pl.BlockSpec(memory_space=pl.ANY)
    return pl.pallas_call(
        mixer_kernel,
        out_shape=(
            shape((rows, channels), bf16),
            shape((rank, channels), f32),
            shape((kinds, rank, channels), f32),
            shape((small, channels), f32),
            shape((shards * groups, taps), f32),
        ),
        in_specs=[pl.BlockSpec(memory_space=pltpu.SMEM), hbm, hbm] + [vmem] * 7,
        out_specs=(hbm,) * 5,
        scratch_shapes=[
            pltpu.VMEM((slabs, shards, kinds, rows, lanes), bf16),
            pltpu.VMEM((slabs, n, lanes), bf16),
            pltpu.VMEM((shards, rank, rows), bf16),
            pltpu.VMEM((shards, 1, rows), i32),
            pltpu.VMEM((slabs, n, lanes), bf16),
            pltpu.VMEM((kinds, rank, c), f32),
            pltpu.VMEM((small, c), f32),
            pltpu.VMEM((groups, taps), f32),
            pltpu.VMEM((rank, n), f32),
            pltpu.VMEM((shards, rank, rows), f32),
            pltpu.VMEM((tps, rank, rows), f32),
            pltpu.VMEM((rank, rows), bf16),
            pltpu.VMEM((shards, rank, rows), bf16),
            pltpu.VMEM((rank, channels), f32),
            pltpu.VMEM((shards, rank, c), f32),
            pltpu.VMEM((rank, c), f32),
            pltpu.VMEM((tps, rank, rows), f32),
            pltpu.VMEM((rank, rows), bf16),
            pltpu.VMEM((n, n), bf16),
            pltpu.VMEM((n, width + LANES), bf16),
            pltpu.VMEM((n + EDGE, width), bf16),
            pltpu.VMEM((n, LANES), bf16),
            pltpu.VMEM((n, width), bf16),
            pltpu.VMEM((n + taps, lanes), bf16),
            pltpu.VMEM((n + taps, lanes), bf16),
            pltpu.VMEM((n + EDGE, width), bf16),
            pltpu.VMEM((groups, wide), f32),
            pltpu.VMEM((groups, wide), f32),
            pltpu.VMEM((groups * taps, wide), bf16),
            pltpu.VMEM((groups * taps, wide), bf16),
            pltpu.VMEM((groups // slabs * taps, wide), f32),
            pltpu.VMEM((n + EDGE, 1), i32),
            pltpu.VMEM((1, n + taps), i32),
            pltpu.SemaphoreType.DMA((9 + 3 * slabs, shards)),
            pltpu.SemaphoreType.DMA((9 + 3 * slabs, shards)),
            pltpu.SemaphoreType.DMA((5 + 3 * slabs,)),
            pltpu.SemaphoreType.DMA((2, tps)),
            pltpu.SemaphoreType.DMA((2, tps)),
        ],
        compiler_params=pltpu.CompilerParams(
            collective_id=0, has_side_effects=True, vmem_limit_bytes=58 * 1024 * 1024
        ),
        cost_estimate=pl.CostEstimate(
            flops=8 * n * groups * taps * wide, bytes_accessed=16 * n * c, transcendentals=0
        ),
    )(lengths, frozen, cot, tokens, down, pos, up, short, long_filter, skip)


def settle_kernel(
    mixer_in, down_in, up_in, small_ref, long_in, mixer_out, down_out, up_out, short_ref, skip_ref, long_out, sems
):
    copies = [
        pltpu.make_async_copy(mixer_in, mixer_out, sems.at[0]),
        pltpu.make_async_copy(down_in, down_out, sems.at[1]),
        pltpu.make_async_copy(up_in, up_out, sems.at[2]),
        pltpu.make_async_copy(long_in, long_out, sems.at[3]),
    ]
    for copy in copies:
        copy.start()
    shorts, kinds, _ = short_ref.shape
    for s in range(shorts):
        short_ref[s] = small_ref[s * kinds : (s + 1) * kinds, :]
    skip_ref[...] = small_ref[shorts * kinds : shorts * kinds + 1, :]
    for copy in copies:
        copy.wait()


def settle(mixer_out, down, up, small, long, shorts, kinds):
    vmem, hbm = pl.BlockSpec(memory_space=pltpu.VMEM), pl.BlockSpec(memory_space=pl.ANY)
    channels = mixer_out.shape[1]
    shape = jax.ShapeDtypeStruct
    same = [shape(array.shape, array.dtype) for array in (mixer_out, down, up, long)]
    return pl.pallas_call(
        settle_kernel,
        out_shape=(
            same[0],
            same[1],
            same[2],
            shape((shorts, kinds, channels), jnp.float32),
            shape((1, channels), jnp.float32),
            same[3],
        ),
        in_specs=[hbm, hbm, hbm, vmem, hbm],
        out_specs=(hbm, hbm, hbm, vmem, vmem, hbm),
        scratch_shapes=[pltpu.SemaphoreType.DMA((4,))],
    )(mixer_out, down, up, small, long)


def by_channels(
    tokens,
    frozen,
    cotangent,
    adapter_down_weight,
    adapter_up_weight,
    short_depthwise_filter,
    long_group_filter,
    skip_direct_scale,
    document_lengths,
    window_row_position,
):
    shorts, kinds, _ = short_depthwise_filter.shape
    mixer_out, grad_down, grad_up, grad_small, grad_long = mixer(
        document_lengths,
        frozen.transpose(1, 0, 2),
        cotangent,
        tokens,
        adapter_down_weight,
        window_row_position[None, :],
        adapter_up_weight.transpose(1, 0, 2),
        short_depthwise_filter,
        long_group_filter,
        skip_direct_scale[None, :],
    )
    mixer_out, grad_down, grad_up, grad_short, grad_skip, grad_long = settle(
        mixer_out, grad_down, grad_up, grad_small, grad_long, shorts, kinds
    )
    return (
        mixer_out,
        grad_down,
        grad_up.transpose(1, 0, 2),
        grad_short,
        grad_long,
        grad_skip[0],
    )


def from_behind(value, axis, steps):
    count = lax.axis_size(axis)
    first, last = (max(0, -steps), min(count, count - steps))
    return lax.ppermute(value, axis, [(source, source + steps) for source in range(first, last)])


def doc_offsets(positions, document_lengths):
    doc_ends = jnp.cumsum(document_lengths)
    starts = doc_ends - document_lengths
    clipped = jnp.maximum(positions, 0)
    begins = jnp.max(jnp.where(starts[None, :] <= clipped[:, None], starts[None, :], 0), axis=1)
    return clipped - begins


def tap_mask(offsets, shift_tap, ndim):
    return (shift_tap <= offsets).astype(jnp.float32).reshape((-1,) + (1,) * (ndim - 1))


def pick_rows(source, row_index):
    padded = jnp.concatenate([source, jnp.zeros((1,) + source.shape[1:], source.dtype)])
    return jnp.take(padded, row_index, axis=0)


def short_apply(extended, filter_taps, offsets):
    length = offsets.shape[0]
    taps = filter_taps.shape[0]
    reach = taps - 1
    running = jnp.zeros((length,) + extended.shape[1:], jnp.float32)
    for shift_tap in range(taps):
        shifted = extended[reach - shift_tap : reach - shift_tap + length].astype(jnp.float32)
        running = running + filter_taps[shift_tap].astype(jnp.float32) * shifted * tap_mask(
            offsets, shift_tap, extended.ndim
        )
    return running


def short_back(back_ext, filter_taps, offsets_ext):
    taps = filter_taps.shape[0]
    length = back_ext.shape[0] - (taps - 1)
    running = jnp.zeros((length,) + back_ext.shape[1:], jnp.float32)
    for shift_tap in range(taps):
        shifted = back_ext[shift_tap : shift_tap + length].astype(jnp.float32)
        masked = shifted * tap_mask(
            offsets_ext[shift_tap : shift_tap + length], shift_tap, back_ext.ndim
        )
        running = running + filter_taps[shift_tap].astype(jnp.float32) * masked
    return running


def short_grad(back_post, pre_ext, offsets, taps):
    length = offsets.shape[0]
    reach = taps - 1
    back_float = back_post.astype(jnp.float32)
    collected = []
    for shift_tap in range(taps):
        shifted = pre_ext[reach - shift_tap : reach - shift_tap + length].astype(jnp.float32)
        collected.append(
            jnp.sum(back_float * shifted * tap_mask(offsets, shift_tap, pre_ext.ndim), axis=0)
        )
    return jnp.stack(collected)


def toeplitz(filter_bank):
    groups = filter_bank.shape[0]
    row_vals = jnp.concatenate(
        [
            jnp.zeros((groups, 1), filter_bank.dtype),
            filter_bank[:, ::-1],
            jnp.zeros((groups, 128), filter_bank.dtype),
        ],
        axis=1,
    )
    tiled = jnp.broadcast_to(row_vals[:, None, :], (groups, 128, 257)).reshape(groups, 128 * 257)
    return tiled[:, : 128 * 256].reshape(groups, 128, 256)


def masked_bank(filter_bank, block_off):
    row_ids = jnp.arange(128, dtype=jnp.int32)[:, None]
    col_ids = jnp.arange(256, dtype=jnp.int32)[None, :]
    allowed = (row_ids + 128 - col_ids <= block_off[:, None]).astype(filter_bank.dtype)
    return filter_bank * allowed[None]


def adapter_hidden(row_tile_block, adapter_down_weight):
    partial_low = lax.dot_general(
        adapter_down_weight,
        row_tile_block,
        (((1,), (1,)), ((), ())),
        preferred_element_type=jnp.float32,
    )
    return lax.psum(partial_low, "tp").astype(jnp.bfloat16)


def on_device(
    tokens,
    frozen,
    cotangent,
    adapter_down_weight,
    adapter_up_weight,
    short_depthwise_filter,
    long_group_filter,
    skip_direct_scale,
    document_lengths,
    window_row_position,
):
    local_rows, channels = tokens.shape
    short_count = short_depthwise_filter.shape[0]
    reach = short_count - 1
    groups = channels // 16
    blocks = local_rows // 128
    shards = lax.axis_size("ctx")
    capacity = 2 * local_rows // shards
    my_index = lax.axis_index("ctx")
    first_pos = my_index * local_rows
    all_pos = lax.all_gather(window_row_position, "ctx", axis=0, tiled=True)
    shard_ids = jnp.arange(shards, dtype=jnp.int32)
    own_dest = window_row_position // local_rows
    own_hits = (own_dest[:, None] == shard_ids[None, :]).astype(jnp.int32)
    own_rank = jnp.sum(jnp.cumsum(own_hits, axis=0) * own_hits, axis=1) - 1
    own_slot = own_dest * capacity + own_rank
    send_rows = (
        jnp.full((shards * capacity,), local_rows, jnp.int32)
        .at[own_slot]
        .set(jnp.arange(local_rows, dtype=jnp.int32))
    )
    grid_pos = all_pos.reshape(shards, local_rows)
    arriving = grid_pos // local_rows == my_index
    arrive_rank = jnp.cumsum(arriving.astype(jnp.int32), axis=1) - 1
    arrive_slot = shard_ids[:, None] * capacity + arrive_rank
    local_target = jnp.where(arriving, grid_pos % local_rows, local_rows)
    recv_rows = (
        jnp.zeros((local_rows,), jnp.int32)
        .at[local_target.reshape(-1)]
        .set(arrive_slot.reshape(-1), mode="drop")
    )
    frozen_buf = pick_rows(frozen, send_rows).reshape((shards, capacity) + frozen.shape[1:])
    token_buf = pick_rows(tokens, send_rows).reshape(shards, capacity, channels)
    got_tokens, got_frozen = (
        lax.all_to_all(token_buf, "ctx", split_axis=0, concat_axis=0, tiled=True),
        lax.all_to_all(frozen_buf, "ctx", split_axis=0, concat_axis=0, tiled=True),
    )
    packed_token_rows = jnp.take(got_tokens.reshape(shards * capacity, channels), recv_rows, axis=0)
    packed_frozen = jnp.take(
        got_frozen.reshape((shards * capacity,) + frozen.shape[1:]), recv_rows, axis=0
    )
    lowrank_product = adapter_hidden(packed_token_rows, adapter_down_weight)
    before_convolution = (
        packed_frozen.astype(jnp.float32)
        + jnp.einsum(
            "ed,ejg->djg", lowrank_product, adapter_up_weight, preferred_element_type=jnp.float32
        )
    ).astype(jnp.bfloat16)
    positions = first_pos - 127 + jnp.arange(local_rows + 255, dtype=jnp.int32)
    offsets_all = doc_offsets(positions, document_lengths)
    own_off = offsets_all[127 : 127 + local_rows]
    pre_edge = from_behind(before_convolution[-reach:], "ctx", 1)
    pre_ext = jnp.concatenate([pre_edge, before_convolution])
    post_conv = short_apply(pre_ext, short_depthwise_filter, own_off).astype(jnp.bfloat16)
    product = (post_conv[:, 1].astype(jnp.float32) * post_conv[:, 2].astype(jnp.float32)).astype(
        jnp.bfloat16
    )
    product_edge = from_behind(product[-127:], "ctx", 1)
    product_ext = jnp.concatenate([jnp.zeros((1, channels), jnp.bfloat16), product_edge, product])
    filter_bank = toeplitz(long_group_filter)
    windows = jnp.concatenate(
        [
            product_ext[:-128].reshape(blocks, 128, channels),
            product_ext[128:].reshape(blocks, 128, channels),
        ],
        axis=1,
    )
    block_offsets = own_off.reshape(blocks, 128)

    def forward_block(pieces):
        window_rows, block_off = pieces
        masked = masked_bank(filter_bank, block_off)
        return jnp.einsum(
            "gij,jgc->igc",
            masked,
            window_rows.reshape(256, groups, 16),
            preferred_element_type=jnp.float32,
        ).reshape(128, channels)

    convolved = lax.map(forward_block, (windows, block_offsets)).reshape(local_rows, channels)
    query_rows = post_conv[:, 0].astype(jnp.float32)
    key_rows = post_conv[:, 1].astype(jnp.float32)
    value_rows = post_conv[:, 2].astype(jnp.float32)
    product_float = product.astype(jnp.float32)
    direct_term = convolved + skip_direct_scale[None, :] * product_float
    mixer_out = (query_rows * direct_term).astype(jnp.bfloat16)
    grad_float = cotangent.astype(jnp.float32)
    gated_back = grad_float * query_rows
    back_conv = gated_back.astype(jnp.bfloat16)
    conv_edge = from_behind(back_conv[:127], "ctx", -1)
    edge_block = jnp.concatenate([conv_edge, jnp.zeros((1, channels), jnp.bfloat16)])

    def backward_block(pieces):
        window_rows, conv_rows, block_off = pieces
        masked = masked_bank(filter_bank, block_off)
        split_conv = conv_rows.reshape(128, groups, 16)
        spread = jnp.einsum(
            "gij,igc->jgc", masked, split_conv, preferred_element_type=jnp.float32
        ).reshape(256, channels)
        pair_sums = jnp.einsum(
            "igc,jgc->gij",
            split_conv,
            window_rows.reshape(256, groups, 16),
            preferred_element_type=jnp.float32,
        )
        skewed = jnp.pad(pair_sums.reshape(groups, 128 * 256), ((0, 0), (0, 128))).reshape(
            groups, 128, 257
        )[:, :, 1:129][:, :, ::-1]
        allowed = (jnp.arange(128, dtype=jnp.int32)[None, :] <= block_off[:, None]).astype(
            jnp.float32
        )
        return (spread, jnp.sum(skewed * allowed[None], axis=1))

    spread_all, filter_parts = lax.map(
        backward_block, (windows, back_conv.reshape(blocks, 128, channels), block_offsets)
    )
    edge_off = offsets_all[127 + local_rows : 127 + local_rows + 128]
    edge_bank = masked_bank(filter_bank, edge_off)[:, :, :128]
    edge_spread = jnp.einsum(
        "gij,igc->jgc",
        edge_bank,
        edge_block.reshape(128, groups, 16),
        preferred_element_type=jnp.float32,
    ).reshape(128, channels)
    following = jnp.concatenate([spread_all[1:, :128], edge_spread[None]], axis=0).reshape(
        local_rows, channels
    )
    product_back = (
        spread_all[:, 128:].reshape(local_rows, channels)
        + following
        + skip_direct_scale[None, :] * gated_back
    )
    grad_long = jnp.sum(filter_parts, axis=0)
    grad_skip = jnp.sum(gated_back * product_float, axis=0)
    query_back = grad_float * direct_term
    back_post = jnp.stack(
        [query_back, product_back * value_rows, product_back * key_rows], axis=1
    ).astype(jnp.bfloat16)
    post_edge = from_behind(back_post[:reach], "ctx", -1)
    back_ext = jnp.concatenate([back_post, post_edge])
    gradient_before_filter = short_back(
        back_ext, short_depthwise_filter, offsets_all[127 : 127 + local_rows + reach]
    ).astype(jnp.bfloat16)
    grad_short = short_grad(back_post, pre_ext, own_off, short_count)
    up_gradient = jnp.einsum(
        "kp,pme->kme", lowrank_product, gradient_before_filter, preferred_element_type=jnp.float32
    )
    partial_gradient = jnp.einsum(
        "ldx,idx->li", adapter_up_weight, gradient_before_filter, preferred_element_type=jnp.float32
    )
    back_low = lax.psum(partial_gradient, "tp").astype(jnp.bfloat16)
    grad_down = jnp.dot(back_low, packed_token_rows, preferred_element_type=jnp.float32)
    summed = lax.psum((grad_down, up_gradient, grad_short, grad_long, grad_skip), "ctx")
    return (mixer_out,) + tuple(summed)


def solution(mesh):
    placed = (
        P("ctx", "tp"),
        P("ctx", None, "tp"),
        P("ctx", "tp"),
        P(None, "tp"),
        P(None, None, "tp"),
        P(None, None, "tp"),
        P("tp", None),
        P("tp"),
        P(),
        P("ctx"),
    )
    channels_each = mesh.shape["ctx"] * LANES

    def run(*args):
        fits = args[0].shape[1] % channels_each == 0
        return (by_channels if fits else on_device)(*args)

    return jax.shard_map(
        run,
        mesh=mesh,
        in_specs=placed,
        out_specs=(
            P("ctx", "tp"),
            P(None, "tp"),
            P(None, None, "tp"),
            P(None, None, "tp"),
            P("tp", None),
            P("tp"),
        ),
        check_vma=False,
    )
```

```python
import functools

import jax
import jax.numpy as jnp
from jax import lax
from jax.experimental import pallas as pl
from jax.experimental.pallas import tpu as pltpu
from jax.sharding import PartitionSpec as P

EDGE = 16
LANES = 128


def fdot(left, right, contract=((1,), (0,))):
    return lax.dot_general(left, right, (contract, ((), ())), preferred_element_type=jnp.float32)


def doc_starts(pos, lengths_ref):
    begins = jnp.zeros_like(pos)
    running = jnp.int32(0)
    for doc in range(lengths_ref.shape[0]):
        begins = jnp.where(pos >= running, running, begins)
        running = running + lengths_ref[doc]
    return begins


def ctx_peers():
    me, count = lax.axis_index("ctx"), lax.axis_size("ctx")
    return me, [(d, lax.rem(me + d, count)) for d in range(1, count)]


def tp_peers():
    me, count = lax.axis_index("tp"), lax.axis_size("tp")
    return me, [(d, lax.rem(me + d, count)) for d in range(1, count)]


def greet():
    barrier = pltpu.get_barrier_semaphore()
    waits = 0
    for axis, (_, peers) in (("ctx", ctx_peers()), ("tp", tp_peers())):
        for _, peer in peers:
            pl.semaphore_signal(
                barrier, inc=1, device_id={axis: peer}, device_id_type=pl.DeviceIdType.MESH
            )
            waits += 1
    pl.semaphore_wait(barrier, waits)


def push(src, dst, send_sem, recv_sem, axis, peer):
    copy = pltpu.make_async_remote_copy(
        src_ref=src,
        dst_ref=dst,
        send_sem=send_sem,
        recv_sem=recv_sem,
        device_id={axis: peer},
        device_id_type=pl.DeviceIdType.MESH,
    )
    copy.start()
    return copy


def part_of(index, size):
    return pl.ds(pl.multiple_of(index * size, size), size)


def mixer_kernel(
    lengths_ref,
    frozen_ref,
    cot_in_ref,
    tokens_ref,
    down_ref,
    pos_ref,
    up_ref,
    short_ref,
    filter_ref,
    skip_ref,
    mixer_out,
    grad_down,
    grad_up,
    grad_small,
    grad_long,
    got_frozen,
    got_cot,
    low_all,
    place_all,
    out_buf,
    up_own,
    small_own,
    long_own,
    back_low,
    low_got,
    back_parts,
    back_own_low,
    back_all,
    down_part,
    down_got,
    down_own,
    low_parts,
    low_own,
    hot_ref,
    rhs,
    pre,
    low_win,
    post,
    prod,
    back,
    back_post,
    taps_f,
    taps_b,
    bank_f,
    bank_b,
    pair_acc,
    start_col,
    start_row,
    send_sems,
    recv_sems,
    own_sems,
    tp_send,
    tp_recv,
):
    slabs, shards, kinds, rows, lanes = got_frozen.shape
    n, c = rows * shards, lanes * slabs
    groups, wide = taps_f.shape
    taps = wide // 2
    per = c // groups
    some = groups // slabs
    width = kinds * lanes
    blocks = n // taps
    shorts = short_ref.shape[0]
    rank = down_ref.shape[0]
    f32, bf16 = jnp.float32, jnp.bfloat16
    me, peers = ctx_peers()
    tp_me, tp_others = tp_peers()
    mine, my_rows = part_of(me, c), part_of(me, rows)
    greet()

    def everyone(step, source, target):
        return [
            push(source(peer), target, send_sems.at[step, d], recv_sems.at[step, d], "ctx", peer)
            for d, peer in peers
        ]

    def tp_swap(step, parts):
        return [
            push(
                parts.at[tp_me],
                parts.at[tp_me],
                tp_send.at[step, d],
                tp_recv.at[step, d],
                "tp",
                peer,
            )
            for d, peer in tp_others
        ]

    def keep(step, source, target):
        copy = pltpu.make_async_copy(source, target, own_sems.at[step])
        copy.start()
        return copy

    def finish(copies):
        for copy in copies:
            copy.wait()

    def tidy(parts, count):
        total = parts[0]
        for t in range(1, count):
            total = total + parts[t]
        return total

    def columns(index, h):
        return pl.ds(pl.multiple_of(index * c + h * lanes, lanes), lanes)

    def fetch_frozen(h):
        own = keep(5 + h, frozen_ref.at[:, :, columns(me, h)], got_frozen.at[h, me])
        return [own] + everyone(
            9 + slabs + h, lambda peer: frozen_ref.at[:, :, columns(peer, h)], got_frozen.at[h, me]
        )

    def fetch_cot(h):
        own = keep(5 + slabs + h, cot_in_ref.at[:, columns(me, h)], got_cot.at[h, my_rows])
        return [own] + everyone(
            9 + 2 * slabs + h,
            lambda peer: cot_in_ref.at[:, columns(peer, h)],
            got_cot.at[h, my_rows],
        )

    places = everyone(1, lambda peer: pos_ref, place_all.at[me])
    coming = fetch_frozen(0)
    place_all[me] = pos_ref[...]
    low_parts[tp_me] = fdot(down_ref[...], tokens_ref[...], ((1,), (1,)))
    swaps = tp_swap(0, low_parts)

    start_col[...] = doc_starts(
        lax.broadcasted_iota(jnp.int32, start_col.shape, 0), lengths_ref
    )
    start_row[...] = doc_starts(
        lax.broadcasted_iota(jnp.int32, start_row.shape, 1), lengths_ref
    )
    finish(swaps)
    low_own[...] = tidy(low_parts, low_parts.shape[0]).astype(bf16)
    low_all[me] = low_own[...]
    lows = everyone(2, lambda peer: low_own, low_all.at[me])

    tap_id = lax.broadcasted_iota(jnp.int32, (taps, wide), 0)
    spot_id = lax.broadcasted_iota(jnp.int32, (taps, wide), 1)
    own_filter = filter_ref[part_of(me, groups), :]
    taps_f[...] = fdot(own_filter, jnp.where(tap_id + spot_id == taps, 1.0, 0.0).astype(bf16))
    taps_b[...] = fdot(own_filter, jnp.where(tap_id == spot_id, 1.0, 0.0).astype(bf16))
    for g in range(groups):
        span = slice(g * taps, (g + 1) * taps)
        for taps_ref, bank in ((taps_f, bank_f), (taps_b, bank_b)):
            line = jnp.broadcast_to(taps_ref[g : g + 1, :], (taps, wide))
            bank[span, :] = pltpu.roll(line, 0, 1, stride=1, stride_axis=0).astype(bf16)
    finish(places)

    @pl.loop(0, shards)
    def _(w):
        base = pl.multiple_of(w * rows, rows)
        spot = lax.broadcasted_iota(jnp.int32, (rows, rows), 0) + base
        for j in range(shards):
            hot_ref[pl.ds(base, rows), j * rows : (j + 1) * rows] = jnp.where(
                place_all[j] == spot, 1.0, 0.0
            ).astype(bf16)

    pre[:EDGE, :] = jnp.zeros((EDGE, width), bf16)
    prod[:taps, :] = jnp.zeros((taps, lanes), bf16)
    back[n:, :] = jnp.zeros((taps, lanes), bf16)
    back_post[n:, :] = jnp.zeros((EDGE, width), bf16)
    small_own[...] = jnp.zeros_like(small_own)
    unit = jnp.where(
        lax.broadcasted_iota(jnp.int32, (rank, LANES), 0)
        == lax.broadcasted_iota(jnp.int32, (rank, LANES), 1),
        1.0,
        0.0,
    ).astype(bf16)
    lane_group = lax.broadcasted_iota(jnp.int32, (taps, lanes), 1) // per
    sel = [jnp.where(lane_group == g, 1.0, 0.0).astype(bf16) for g in range(some)]
    turned = wide - 1 - lax.broadcasted_iota(jnp.int32, (taps, wide), 1)
    flip = jnp.where(
        lax.broadcasted_iota(jnp.int32, (wide, wide), 0)
        + lax.broadcasted_iota(jnp.int32, (wide, wide), 1)
        == wide - 1,
        1.0,
        0.0,
    ).astype(bf16)

    def pick(stacked):
        chosen = stacked[:taps]
        for g in range(1, some):
            chosen = jnp.where(lane_group == g, stacked[g * taps : (g + 1) * taps], chosen)
        return chosen

    finish(lows)
    outs = []
    for h in range(slabs):
        frozens = coming
        here = columns(me, h)
        slab = slice(h * lanes, (h + 1) * lanes)
        bank_rows = slice(h * some * taps, (h + 1) * some * taps)
        short_rows = []
        for s in range(shorts):
            lines = short_ref[s, :, here].astype(f32)
            short_rows.append(
                jnp.concatenate([lines[a : a + 1] for a in range(kinds)], axis=1)
            )
        up_parts = [up_ref[a, :, here] for a in range(kinds)]
        skip = skip_ref[:, here]

        for d in range(shards):
            frozens[d].wait()
            j = lax.rem(me + shards - d, shards)
            at = part_of(j, rows)
            low = low_all[j]
            for a in range(kinds):
                cols = slice(a * lanes, (a + 1) * lanes)
                rhs[at, cols] = (
                    got_frozen[h, j, a].astype(f32) + fdot(low, up_parts[a], ((0,), (0,)))
                ).astype(bf16)
            if h == 0:
                rhs[at, width:] = fdot(low, unit, ((0,), (0,))).astype(bf16)
        if h == 0:
            cots = fetch_cot(0)
        tall = rows * 2

        @pl.loop(0, n // tall)
        def _(w):
            base = pl.multiple_of(w * tall, tall)
            at = pl.ds(base, tall)
            to = pl.ds(pl.multiple_of(base + EDGE, EDGE), tall)
            if h == 0:
                moved = fdot(hot_ref[at, :], rhs[...]).astype(bf16)
                pre[to, :] = moved[:, :width]
                low_win[at, :] = moved[:, width:]
            else:
                pre[to, :] = fdot(hot_ref[at, :], rhs[:, :width]).astype(bf16)

        finish(cots)
        if h + 1 < slabs:
            coming = fetch_frozen(h + 1)
            cots = fetch_cot(h + 1)

        @pl.loop(0, blocks)
        def _(b):
            base = pl.multiple_of(b * taps, taps)
            at = pl.ds(base, taps)
            ext = pre[pl.ds(base, taps + EDGE), :].astype(f32)
            off = lax.broadcasted_iota(jnp.int32, (taps, 1), 0) + base - start_col[at, :]
            total = jnp.zeros((taps, width), f32)
            for s in range(shorts):
                gate = (off >= s).astype(f32)
                total = total + short_rows[s] * ext[EDGE - s : EDGE - s + taps] * gate
            rounded = total.astype(bf16)
            post[at, :] = rounded
            rounded = rounded.astype(f32)
            prod[pl.ds(pl.multiple_of(base + taps, taps), taps), :] = (
                rounded[:, lanes : 2 * lanes] * rounded[:, 2 * lanes :]
            ).astype(bf16)
            back[at, :] = (got_cot[h, at, :].astype(f32) * rounded[:, :lanes]).astype(bf16)

        pair_acc[...] = jnp.zeros_like(pair_acc)

        @pl.loop(0, blocks)
        def _(b):
            base = pl.multiple_of(b * taps, taps)
            at = pl.ds(base, taps)
            window = prod[pl.ds(base, 2 * taps), :]
            ahead = back[pl.ds(base, 2 * taps), :]
            begin = start_col[at, :]
            col_pos = lax.broadcasted_iota(jnp.int32, (taps, wide), 1) + (base - taps)
            gate_f = jnp.where(col_pos >= begin, 1.0, 0.0).astype(bf16)
            gate_r = jnp.where(turned + (base - taps) >= begin, 1.0, 0.0)
            row_pos = lax.broadcasted_iota(jnp.int32, (taps, wide), 0) + base
            gate_b = jnp.where(row_pos >= start_row[:, pl.ds(base, wide)], 1.0, 0.0).astype(bf16)
            many_f = jnp.concatenate([gate_f] * some, axis=0)
            many_b = jnp.concatenate([gate_b] * some, axis=0)
            conv = pick(fdot(bank_f[bank_rows, :] * many_f, window))
            spread = pick(fdot(bank_b[bank_rows, :] * many_b, ahead))
            back_here = ahead[:taps]
            split = jnp.concatenate([back_here * sel[g] for g in range(some)], axis=0)
            pairs = fdot(split, fdot(flip, window).astype(bf16), ((1,), (1,)))
            for g in range(some):
                span = slice(g * taps, (g + 1) * taps)
                pair_acc[span, :] += pairs[span] * gate_r
            product = window[taps:].astype(f32)
            cot = got_cot[h, at, :].astype(f32)
            query = post[at, :lanes].astype(f32)
            key = post[at, lanes : 2 * lanes].astype(f32)
            value = post[at, 2 * lanes :].astype(f32)
            gated = cot * query
            direct = conv + skip * product
            out_buf[h, at, :] = (query * direct).astype(bf16)
            product_back = spread + skip * gated
            skip_row = shorts * kinds
            small_own[skip_row : skip_row + 1, slab] += jnp.sum(gated * product, axis=0, keepdims=True)
            back_post[at, :lanes] = (cot * direct).astype(bf16)
            back_post[at, lanes : 2 * lanes] = (product_back * value).astype(bf16)
            back_post[at, 2 * lanes :] = (product_back * key).astype(bf16)

        outs += everyone(
            9 + h, lambda peer: out_buf.at[h, part_of(peer, rows)], mixer_out.at[:, here]
        )
        outs.append(keep(5 + 2 * slabs + h, out_buf.at[h, my_rows], mixer_out.at[:, here]))

        @pl.loop(0, blocks)
        def _(b):
            base = pl.multiple_of(b * taps, taps)
            at = pl.ds(base, taps)
            ext = pre[pl.ds(base, taps + EDGE), :].astype(f32)
            back_ext = back_post[pl.ds(base, taps + EDGE), :].astype(f32)
            off = (
                lax.broadcasted_iota(jnp.int32, (taps + EDGE, 1), 0)
                + base
                - start_col[pl.ds(base, taps + EDGE), :]
            )
            total = jnp.zeros((taps, width), f32)
            for s in range(shorts):
                masked = back_ext * (off >= s).astype(f32)
                total = total + short_rows[s] * masked[s : s + taps]
                sums = jnp.sum(
                    masked[:taps] * ext[EDGE - s : EDGE - s + taps], axis=0, keepdims=True
                )
                for a in range(kinds):
                    row = s * kinds + a
                    small_own[row : row + 1, slab] += sums[:, a * lanes : (a + 1) * lanes]
            rhs[at, :width] = total.astype(bf16)

        back_pre = rhs[:, :width]
        low_term = fdot(jnp.concatenate(up_parts, axis=1), back_pre, ((1,), (1,)))
        back_low[...] = low_term if h == 0 else back_low[...] + low_term
        if h + 1 == slabs:
            reduce_low = everyone(0, lambda peer: back_low.at[:, part_of(peer, rows)], low_got.at[me])
            low_got[me] = back_low[:, my_rows]
        up_term = fdot(low_win[...], back_pre, ((0,), (0,)))
        for a in range(kinds):
            up_own[a, :, slab] = up_term[:rank, a * lanes : (a + 1) * lanes]

        for g in range(some):
            span = slice(g * taps, (g + 1) * taps)
            square = pltpu.roll(pair_acc[span, :], wide - taps + 1, 1, stride=1, stride_axis=0)
            row = h * some + g
            long_own[row : row + 1, :] = jnp.sum(square[:, :taps], axis=0, keepdims=True)

    copies = everyone(3, lambda peer: up_own, grad_up.at[:, :, mine])
    copies += everyone(4, lambda peer: small_own, grad_small.at[:, mine])
    copies += everyone(5, lambda peer: long_own, grad_long.at[part_of(me, groups)])
    copies += outs
    copies.append(keep(1, up_own, grad_up.at[:, :, mine]))
    copies.append(keep(2, small_own, grad_small.at[:, mine]))
    copies.append(keep(3, long_own, grad_long.at[part_of(me, groups)]))
    finish(reduce_low)
    back_parts[tp_me] = tidy(low_got, shards)
    finish(tp_swap(1, back_parts))
    back_own_low[...] = tidy(back_parts, back_parts.shape[0]).astype(bf16)
    back_all[me] = back_own_low[...]
    finish(everyone(6, lambda peer: back_own_low, back_all.at[me]))
    back_own = jnp.zeros((rank, rows), f32)
    for j in range(shards):
        spot = lax.broadcasted_iota(jnp.int32, (rows, rows), 0) + j * rows
        hot = jnp.where(pos_ref[...] == spot, 1.0, 0.0).astype(bf16)
        back_own = back_own + fdot(back_all[j], hot)
    down_part[...] = fdot(back_own.astype(bf16), tokens_ref[...])
    reduce_down = everyone(7, lambda peer: down_part.at[:, part_of(peer, c)], down_got.at[me])
    down_got[me] = down_part[:, mine]
    finish(reduce_down)
    down_own[...] = tidy(down_got, shards)
    copies += everyone(8, lambda peer: down_own, grad_down.at[:, mine])
    copies.append(keep(4, down_own, grad_down.at[:, mine]))
    finish(copies)


def mixer(lengths, frozen, cot, tokens, down, pos, up, short, long_filter, skip):
    kinds, rows, channels = frozen.shape
    shards, tps = lax.axis_size("ctx"), lax.axis_size("tp")
    n, c = rows * shards, channels // shards
    slabs, lanes = c // LANES, LANES
    taps = long_filter.shape[1]
    groups, wide = long_filter.shape[0] // shards, 2 * taps
    width = kinds * lanes
    rank = down.shape[0]
    small = -(-(short.shape[0] * kinds + 1) // 8) * 8
    f32, bf16, i32 = jnp.float32, jnp.bfloat16, jnp.int32
    shape = jax.ShapeDtypeStruct
    vmem, hbm = pl.BlockSpec(memory_space=pltpu.VMEM), pl.BlockSpec(memory_space=pl.ANY)
    return pl.pallas_call(
        mixer_kernel,
        out_shape=(
            shape((rows, channels), bf16),
            shape((rank, channels), f32),
            shape((kinds, rank, channels), f32),
            shape((small, channels), f32),
            shape((shards * groups, taps), f32),
        ),
        in_specs=[pl.BlockSpec(memory_space=pltpu.SMEM), hbm, hbm] + [vmem] * 7,
        out_specs=(hbm,) * 5,
        scratch_shapes=[
            pltpu.VMEM((slabs, shards, kinds, rows, lanes), bf16),
            pltpu.VMEM((slabs, n, lanes), bf16),
            pltpu.VMEM((shards, rank, rows), bf16),
            pltpu.VMEM((shards, 1, rows), i32),
            pltpu.VMEM((slabs, n, lanes), bf16),
            pltpu.VMEM((kinds, rank, c), f32),
            pltpu.VMEM((small, c), f32),
            pltpu.VMEM((groups, taps), f32),
            pltpu.VMEM((rank, n), f32),
            pltpu.VMEM((shards, rank, rows), f32),
            pltpu.VMEM((tps, rank, rows), f32),
            pltpu.VMEM((rank, rows), bf16),
            pltpu.VMEM((shards, rank, rows), bf16),
            pltpu.VMEM((rank, channels), f32),
            pltpu.VMEM((shards, rank, c), f32),
            pltpu.VMEM((rank, c), f32),
            pltpu.VMEM((tps, rank, rows), f32),
            pltpu.VMEM((rank, rows), bf16),
            pltpu.VMEM((n, n), bf16),
            pltpu.VMEM((n, width + LANES), bf16),
            pltpu.VMEM((n + EDGE, width), bf16),
            pltpu.VMEM((n, LANES), bf16),
            pltpu.VMEM((n, width), bf16),
            pltpu.VMEM((n + taps, lanes), bf16),
            pltpu.VMEM((n + taps, lanes), bf16),
            pltpu.VMEM((n + EDGE, width), bf16),
            pltpu.VMEM((groups, wide), f32),
            pltpu.VMEM((groups, wide), f32),
            pltpu.VMEM((groups * taps, wide), bf16),
            pltpu.VMEM((groups * taps, wide), bf16),
            pltpu.VMEM((groups // slabs * taps, wide), f32),
            pltpu.VMEM((n + EDGE, 1), i32),
            pltpu.VMEM((1, n + taps), i32),
            pltpu.SemaphoreType.DMA((9 + 3 * slabs, shards)),
            pltpu.SemaphoreType.DMA((9 + 3 * slabs, shards)),
            pltpu.SemaphoreType.DMA((5 + 3 * slabs,)),
            pltpu.SemaphoreType.DMA((2, tps)),
            pltpu.SemaphoreType.DMA((2, tps)),
        ],
        compiler_params=pltpu.CompilerParams(
            collective_id=0, has_side_effects=True, vmem_limit_bytes=58 * 1024 * 1024
        ),
        cost_estimate=pl.CostEstimate(
            flops=8 * n * groups * taps * wide, bytes_accessed=16 * n * c, transcendentals=0
        ),
    )(lengths, frozen, cot, tokens, down, pos, up, short, long_filter, skip)


def settle_kernel(
    mixer_in, down_in, up_in, small_ref, long_in, mixer_out, down_out, up_out, short_ref, skip_ref, long_out
):
    for source, target in (
        (mixer_in, mixer_out),
        (down_in, down_out),
        (up_in, up_out),
        (long_in, long_out),
    ):
        target[...] = source[...]
    shorts, kinds, _ = short_ref.shape
    for s in range(shorts):
        short_ref[s] = small_ref[s * kinds : (s + 1) * kinds, :]
    skip_ref[...] = small_ref[shorts * kinds : shorts * kinds + 1, :]


def settle(mixer_out, down, up, small, long, shorts, kinds):
    vmem = pl.BlockSpec(memory_space=pltpu.VMEM)
    channels = mixer_out.shape[1]
    shape = jax.ShapeDtypeStruct
    same = [shape(array.shape, array.dtype) for array in (mixer_out, down, up, long)]
    return pl.pallas_call(
        settle_kernel,
        out_shape=(
            same[0],
            same[1],
            same[2],
            shape((shorts, kinds, channels), jnp.float32),
            shape((1, channels), jnp.float32),
            same[3],
        ),
        in_specs=[vmem] * 5,
        out_specs=(vmem,) * 6,
        compiler_params=pltpu.CompilerParams(vmem_limit_bytes=16 * 1024 * 1024),
    )(mixer_out, down, up, small, long)


def by_channels(
    tokens,
    frozen,
    cotangent,
    adapter_down_weight,
    adapter_up_weight,
    short_depthwise_filter,
    long_group_filter,
    skip_direct_scale,
    document_lengths,
    window_row_position,
):
    shorts, kinds, _ = short_depthwise_filter.shape
    mixer_out, grad_down, grad_up, grad_small, grad_long = mixer(
        document_lengths,
        frozen.transpose(1, 0, 2),
        cotangent,
        tokens,
        adapter_down_weight,
        window_row_position[None, :],
        adapter_up_weight.transpose(1, 0, 2),
        short_depthwise_filter,
        long_group_filter,
        skip_direct_scale[None, :],
    )
    mixer_out, grad_down, grad_up, grad_short, grad_skip, grad_long = settle(
        mixer_out, grad_down, grad_up, grad_small, grad_long, shorts, kinds
    )
    return (
        mixer_out,
        grad_down,
        grad_up.transpose(1, 0, 2),
        grad_short,
        grad_long,
        grad_skip[0],
    )


def from_behind(value, axis, steps):
    count = lax.axis_size(axis)
    first, last = (max(0, -steps), min(count, count - steps))
    return lax.ppermute(value, axis, [(source, source + steps) for source in range(first, last)])


def doc_offsets(positions, document_lengths):
    doc_ends = jnp.cumsum(document_lengths)
    starts = doc_ends - document_lengths
    clipped = jnp.maximum(positions, 0)
    begins = jnp.max(jnp.where(starts[None, :] <= clipped[:, None], starts[None, :], 0), axis=1)
    return clipped - begins


def tap_mask(offsets, shift_tap, ndim):
    return (shift_tap <= offsets).astype(jnp.float32).reshape((-1,) + (1,) * (ndim - 1))


def pick_rows(source, row_index):
    padded = jnp.concatenate([source, jnp.zeros((1,) + source.shape[1:], source.dtype)])
    return jnp.take(padded, row_index, axis=0)


def short_apply(extended, filter_taps, offsets):
    length = offsets.shape[0]
    taps = filter_taps.shape[0]
    reach = taps - 1
    running = jnp.zeros((length,) + extended.shape[1:], jnp.float32)
    for shift_tap in range(taps):
        shifted = extended[reach - shift_tap : reach - shift_tap + length].astype(jnp.float32)
        running = running + filter_taps[shift_tap].astype(jnp.float32) * shifted * tap_mask(
            offsets, shift_tap, extended.ndim
        )
    return running


def short_back(back_ext, filter_taps, offsets_ext):
    taps = filter_taps.shape[0]
    length = back_ext.shape[0] - (taps - 1)
    running = jnp.zeros((length,) + back_ext.shape[1:], jnp.float32)
    for shift_tap in range(taps):
        shifted = back_ext[shift_tap : shift_tap + length].astype(jnp.float32)
        masked = shifted * tap_mask(
            offsets_ext[shift_tap : shift_tap + length], shift_tap, back_ext.ndim
        )
        running = running + filter_taps[shift_tap].astype(jnp.float32) * masked
    return running


def short_grad(back_post, pre_ext, offsets, taps):
    length = offsets.shape[0]
    reach = taps - 1
    back_float = back_post.astype(jnp.float32)
    collected = []
    for shift_tap in range(taps):
        shifted = pre_ext[reach - shift_tap : reach - shift_tap + length].astype(jnp.float32)
        collected.append(
            jnp.sum(back_float * shifted * tap_mask(offsets, shift_tap, pre_ext.ndim), axis=0)
        )
    return jnp.stack(collected)


def toeplitz(filter_bank):
    groups = filter_bank.shape[0]
    row_vals = jnp.concatenate(
        [
            jnp.zeros((groups, 1), filter_bank.dtype),
            filter_bank[:, ::-1],
            jnp.zeros((groups, 128), filter_bank.dtype),
        ],
        axis=1,
    )
    tiled = jnp.broadcast_to(row_vals[:, None, :], (groups, 128, 257)).reshape(groups, 128 * 257)
    return tiled[:, : 128 * 256].reshape(groups, 128, 256)


def masked_bank(filter_bank, block_off):
    row_ids = jnp.arange(128, dtype=jnp.int32)[:, None]
    col_ids = jnp.arange(256, dtype=jnp.int32)[None, :]
    allowed = (row_ids + 128 - col_ids <= block_off[:, None]).astype(filter_bank.dtype)
    return filter_bank * allowed[None]


def adapter_hidden(row_tile_block, adapter_down_weight):
    partial_low = lax.dot_general(
        adapter_down_weight,
        row_tile_block,
        (((1,), (1,)), ((), ())),
        preferred_element_type=jnp.float32,
    )
    return lax.psum(partial_low, "tp").astype(jnp.bfloat16)


def on_device(
    tokens,
    frozen,
    cotangent,
    adapter_down_weight,
    adapter_up_weight,
    short_depthwise_filter,
    long_group_filter,
    skip_direct_scale,
    document_lengths,
    window_row_position,
):
    local_rows, channels = tokens.shape
    short_count = short_depthwise_filter.shape[0]
    reach = short_count - 1
    groups = channels // 16
    blocks = local_rows // 128
    shards = lax.axis_size("ctx")
    capacity = 2 * local_rows // shards
    my_index = lax.axis_index("ctx")
    first_pos = my_index * local_rows
    all_pos = lax.all_gather(window_row_position, "ctx", axis=0, tiled=True)
    shard_ids = jnp.arange(shards, dtype=jnp.int32)
    own_dest = window_row_position // local_rows
    own_hits = (own_dest[:, None] == shard_ids[None, :]).astype(jnp.int32)
    own_rank = jnp.sum(jnp.cumsum(own_hits, axis=0) * own_hits, axis=1) - 1
    own_slot = own_dest * capacity + own_rank
    send_rows = (
        jnp.full((shards * capacity,), local_rows, jnp.int32)
        .at[own_slot]
        .set(jnp.arange(local_rows, dtype=jnp.int32))
    )
    grid_pos = all_pos.reshape(shards, local_rows)
    arriving = grid_pos // local_rows == my_index
    arrive_rank = jnp.cumsum(arriving.astype(jnp.int32), axis=1) - 1
    arrive_slot = shard_ids[:, None] * capacity + arrive_rank
    local_target = jnp.where(arriving, grid_pos % local_rows, local_rows)
    recv_rows = (
        jnp.zeros((local_rows,), jnp.int32)
        .at[local_target.reshape(-1)]
        .set(arrive_slot.reshape(-1), mode="drop")
    )
    frozen_buf = pick_rows(frozen, send_rows).reshape((shards, capacity) + frozen.shape[1:])
    token_buf = pick_rows(tokens, send_rows).reshape(shards, capacity, channels)
    got_tokens, got_frozen = (
        lax.all_to_all(token_buf, "ctx", split_axis=0, concat_axis=0, tiled=True),
        lax.all_to_all(frozen_buf, "ctx", split_axis=0, concat_axis=0, tiled=True),
    )
    packed_token_rows = jnp.take(got_tokens.reshape(shards * capacity, channels), recv_rows, axis=0)
    packed_frozen = jnp.take(
        got_frozen.reshape((shards * capacity,) + frozen.shape[1:]), recv_rows, axis=0
    )
    lowrank_product = adapter_hidden(packed_token_rows, adapter_down_weight)
    before_convolution = (
        packed_frozen.astype(jnp.float32)
        + jnp.einsum(
            "ed,ejg->djg", lowrank_product, adapter_up_weight, preferred_element_type=jnp.float32
        )
    ).astype(jnp.bfloat16)
    positions = first_pos - 127 + jnp.arange(local_rows + 255, dtype=jnp.int32)
    offsets_all = doc_offsets(positions, document_lengths)
    own_off = offsets_all[127 : 127 + local_rows]
    pre_edge = from_behind(before_convolution[-reach:], "ctx", 1)
    pre_ext = jnp.concatenate([pre_edge, before_convolution])
    post_conv = short_apply(pre_ext, short_depthwise_filter, own_off).astype(jnp.bfloat16)
    product = (post_conv[:, 1].astype(jnp.float32) * post_conv[:, 2].astype(jnp.float32)).astype(
        jnp.bfloat16
    )
    product_edge = from_behind(product[-127:], "ctx", 1)
    product_ext = jnp.concatenate([jnp.zeros((1, channels), jnp.bfloat16), product_edge, product])
    filter_bank = toeplitz(long_group_filter)
    windows = jnp.concatenate(
        [
            product_ext[:-128].reshape(blocks, 128, channels),
            product_ext[128:].reshape(blocks, 128, channels),
        ],
        axis=1,
    )
    block_offsets = own_off.reshape(blocks, 128)

    def forward_block(pieces):
        window_rows, block_off = pieces
        masked = masked_bank(filter_bank, block_off)
        return jnp.einsum(
            "gij,jgc->igc",
            masked,
            window_rows.reshape(256, groups, 16),
            preferred_element_type=jnp.float32,
        ).reshape(128, channels)

    convolved = lax.map(forward_block, (windows, block_offsets)).reshape(local_rows, channels)
    query_rows = post_conv[:, 0].astype(jnp.float32)
    key_rows = post_conv[:, 1].astype(jnp.float32)
    value_rows = post_conv[:, 2].astype(jnp.float32)
    product_float = product.astype(jnp.float32)
    direct_term = convolved + skip_direct_scale[None, :] * product_float
    mixer_out = (query_rows * direct_term).astype(jnp.bfloat16)
    grad_float = cotangent.astype(jnp.float32)
    gated_back = grad_float * query_rows
    back_conv = gated_back.astype(jnp.bfloat16)
    conv_edge = from_behind(back_conv[:127], "ctx", -1)
    edge_block = jnp.concatenate([conv_edge, jnp.zeros((1, channels), jnp.bfloat16)])

    def backward_block(pieces):
        window_rows, conv_rows, block_off = pieces
        masked = masked_bank(filter_bank, block_off)
        split_conv = conv_rows.reshape(128, groups, 16)
        spread = jnp.einsum(
            "gij,igc->jgc", masked, split_conv, preferred_element_type=jnp.float32
        ).reshape(256, channels)
        pair_sums = jnp.einsum(
            "igc,jgc->gij",
            split_conv,
            window_rows.reshape(256, groups, 16),
            preferred_element_type=jnp.float32,
        )
        skewed = jnp.pad(pair_sums.reshape(groups, 128 * 256), ((0, 0), (0, 128))).reshape(
            groups, 128, 257
        )[:, :, 1:129][:, :, ::-1]
        allowed = (jnp.arange(128, dtype=jnp.int32)[None, :] <= block_off[:, None]).astype(
            jnp.float32
        )
        return (spread, jnp.sum(skewed * allowed[None], axis=1))

    spread_all, filter_parts = lax.map(
        backward_block, (windows, back_conv.reshape(blocks, 128, channels), block_offsets)
    )
    edge_off = offsets_all[127 + local_rows : 127 + local_rows + 128]
    edge_bank = masked_bank(filter_bank, edge_off)[:, :, :128]
    edge_spread = jnp.einsum(
        "gij,igc->jgc",
        edge_bank,
        edge_block.reshape(128, groups, 16),
        preferred_element_type=jnp.float32,
    ).reshape(128, channels)
    following = jnp.concatenate([spread_all[1:, :128], edge_spread[None]], axis=0).reshape(
        local_rows, channels
    )
    product_back = (
        spread_all[:, 128:].reshape(local_rows, channels)
        + following
        + skip_direct_scale[None, :] * gated_back
    )
    grad_long = jnp.sum(filter_parts, axis=0)
    grad_skip = jnp.sum(gated_back * product_float, axis=0)
    query_back = grad_float * direct_term
    back_post = jnp.stack(
        [query_back, product_back * value_rows, product_back * key_rows], axis=1
    ).astype(jnp.bfloat16)
    post_edge = from_behind(back_post[:reach], "ctx", -1)
    back_ext = jnp.concatenate([back_post, post_edge])
    gradient_before_filter = short_back(
        back_ext, short_depthwise_filter, offsets_all[127 : 127 + local_rows + reach]
    ).astype(jnp.bfloat16)
    grad_short = short_grad(back_post, pre_ext, own_off, short_count)
    up_gradient = jnp.einsum(
        "kp,pme->kme", lowrank_product, gradient_before_filter, preferred_element_type=jnp.float32
    )
    partial_gradient = jnp.einsum(
        "ldx,idx->li", adapter_up_weight, gradient_before_filter, preferred_element_type=jnp.float32
    )
    back_low = lax.psum(partial_gradient, "tp").astype(jnp.bfloat16)
    grad_down = jnp.dot(back_low, packed_token_rows, preferred_element_type=jnp.float32)
    summed = lax.psum((grad_down, up_gradient, grad_short, grad_long, grad_skip), "ctx")
    return (mixer_out,) + tuple(summed)


def solution(mesh):
    placed = (
        P("ctx", "tp"),
        P("ctx", None, "tp"),
        P("ctx", "tp"),
        P(None, "tp"),
        P(None, None, "tp"),
        P(None, None, "tp"),
        P("tp", None),
        P("tp"),
        P(),
        P("ctx"),
    )
    channels_each = mesh.shape["ctx"] * LANES

    def run(*args):
        fits = args[0].shape[1] % channels_each == 0
        return (by_channels if fits else on_device)(*args)

    return jax.shard_map(
        run,
        mesh=mesh,
        in_specs=placed,
        out_specs=(
            P("ctx", "tp"),
            P(None, "tp"),
            P(None, None, "tp"),
            P(None, None, "tp"),
            P("tp", None),
            P("tp"),
        ),
        check_vma=False,
    )
```
